256 devices in a mesh: row: 16 (over z, y_lo), col: 16 (over y_hi, x, core).
Axes of the slice: x: 4, y: 4 (y_hi: 2, y_lo: 2; y = y_hi * 2 + y_lo), z: 8, core: 2. Of those that a mesh axis runs over, the one named last changes fastest.
Arguments:
- rho_re: float32 [4096, 4096], P('row', 'col'), may hold values from -6 to 6
- rho_im: float32 [4096, 4096], P('row', 'col'), may hold values from -6 to 6
- diag_re: bfloat16 [16, 256, 256], P('col'), may hold values from -0.21875 to 0.21875
- diag_im: bfloat16 [16, 256, 256], P('col'), may hold values from -0.21875 to 0.21875
- coupling_re: bfloat16 [16, 256, 256], P('col'), may hold values from -0.21875 to 0.21875
- coupling_im: bfloat16 [16, 256, 256], P('col'), may hold values from -0.21875 to 0.21875
- inject_re: bfloat16 [16, 256, 256], P('col'), may hold values from -0.375 to 0.375
- inject_im: bfloat16 [16, 256, 256], P('col'), may hold values from -0.375 to 0.375
- dephasing: float32 [4096], replicated, may hold values from 0.2 to 2
- lead_slice: int32 [4], replicated, may hold values from 0 to 15
- lead_slot: int32 [4], replicated, may hold values from 0 to 15
Outputs:
- prop_re: float32 [4096, 4096], P('row', 'col')
- prop_im: float32 [4096, 4096], P('row', 'col')
The draws below stay inside these ranges and needn't reach their ends.
Inputs may be any that keep to these rules, and one draw needn't show every extreme that they name: lead_slice holds slice numbers of the window, 0 to 15; several contacts may share a slice. lead_slot holds numbers of stored injection blocks, 0 to 15; several contacts may share a block.
All inputs are finite; a program needn't handle non-finite values.
Results may differ from the reference program's by a relative error of at most 0.0032.
Values may be sent and summed in bfloat16 or wider, within the bound.
A program may use at most 64 MiB of HBM per device.

```python
import math
import jax
import jax.numpy as jnp
from jax import lax

S = 256
LEADS = 4
NSLICE = 16
N = 4096
BLOCKS = 16


def touch_ends(result, key, low, largest):
    index_at = [jax.random.randint(jax.random.fold_in(key, axis), (), 0, length) for axis, length in enumerate(result.shape)]
    main_axis = result.shape.index(max(result.shape))
    neighbour = index_at[:main_axis] + [(index_at[main_axis] + 1) % result.shape[main_axis]] + index_at[main_axis + 1:]
    return result.at[tuple(index_at)].set(low).at[tuple(neighbour)].set(largest)


def block_scale(own_key, shape, cuts, least, largest):
    def one(axis_at, blocks):
        heights = jax.random.uniform(jax.random.fold_in(jax.random.fold_in(own_key, 6), axis_at), (blocks,), jnp.float32, least / len(cuts), largest / len(cuts))
        return jnp.repeat(jnp.exp(heights), shape[axis_at] // blocks).reshape((-1,) + (1,) * (len(shape) - axis_at - 1))

    level = one(*cuts[0])
    for cut in cuts[1:]:
        level = level * one(*cut)
    return level


def bell_draw(own_key, shape, deviation, limit, shards=(), dtype=jnp.bfloat16):
    loudness = block_scale(own_key, shape, shards, -0.22, 0.18) if shards else 1.0
    values = jax.random.normal(own_key, shape, jnp.float32) * deviation * loudness
    return jnp.minimum(jnp.maximum(values, -limit), limit).astype(dtype)


def setup_inputs(seed: int = 0) -> dict:
    key_of = jax.random.split(jax.random.key(seed), 12)
    rho_re = bell_draw(key_of[0], (N, N), 1.0, 6.0, ((0, 16), (1, 16)), jnp.float32)
    rho_im = bell_draw(key_of[1], (N, N), 1.0, 6.0, ((0, 16), (1, 16)), jnp.float32)
    diag_re = bell_draw(key_of[2], (NSLICE, S, S), (3 * S) ** -0.5, 0.21875, ((0, 16),))
    diag_im = bell_draw(key_of[3], (NSLICE, S, S), (3 * S) ** -0.5, 0.21875, ((0, 16),))
    coupling_re = bell_draw(key_of[4], (NSLICE, S, S), (3 * S) ** -0.5, 0.21875, ((0, 16),))
    coupling_im = bell_draw(key_of[5], (NSLICE, S, S), (3 * S) ** -0.5, 0.21875, ((0, 16),))
    inject_re = bell_draw(key_of[6], (BLOCKS, S, S), S ** -0.5, 0.375, ((0, 16),))
    inject_im = bell_draw(key_of[7], (BLOCKS, S, S), S ** -0.5, 0.375, ((0, 16),))
    dephasing = jnp.clip(jnp.exp(jax.random.uniform(key_of[8], (N,), jnp.float32, math.log(0.2), math.log(2.0))), 0.2, 2.0)
    lead_slice = touch_ends(jax.random.randint(key_of[9], (LEADS,), 0, NSLICE), jax.random.fold_in(key_of[9], 1), 0, NSLICE - 1).astype(jnp.int32)
    lead_slot = touch_ends(jax.random.randint(key_of[10], (LEADS,), 0, BLOCKS), jax.random.fold_in(key_of[10], 1), 0, BLOCKS - 1).astype(jnp.int32)
    return {"rho_re": rho_re, "rho_im": rho_im, "diag_re": diag_re, "diag_im": diag_im, "coupling_re": coupling_re, "coupling_im": coupling_im, "inject_re": inject_re, "inject_im": inject_im, "dephasing": dephasing, "lead_slice": lead_slice, "lead_slot": lead_slot}


step_scale = 0.25
coeff_zero = 0.7652
coeff_one = 0.8801
coeff_two = 0.2298


def hermitian(part_re, part_im):
    sym_re = 0.5 * (part_re.astype(jnp.float32) + jnp.swapaxes(part_re, -1, -2).astype(jnp.float32))
    sym_im = 0.5 * (part_im.astype(jnp.float32) - jnp.swapaxes(part_im, -1, -2).astype(jnp.float32))
    return sym_re.astype(jnp.bfloat16), sym_im.astype(jnp.bfloat16)


def block_left(form, block_re, block_im, data_re, data_im, conj_flag):
    sign_value = -1.0 if conj_flag else 1.0
    first_re = block_re.astype(jnp.float32)
    first_im = sign_value * block_im.astype(jnp.float32)
    out_re = jnp.einsum(form, first_re, data_re) - jnp.einsum(form, first_im, data_im)
    out_im = jnp.einsum(form, first_re, data_im) + jnp.einsum(form, first_im, data_re)
    return out_re, out_im


def block_right(form, data_re, data_im, block_re, block_im, conj_flag):
    sign_value = -1.0 if conj_flag else 1.0
    second_re = block_re.astype(jnp.float32)
    second_im = sign_value * block_im.astype(jnp.float32)
    out_re = jnp.einsum(form, data_re, second_re) - jnp.einsum(form, data_im, second_im)
    out_im = jnp.einsum(form, data_re, second_im) + jnp.einsum(form, data_im, second_re)
    return out_re, out_im


def generator(field_re, field_im, diag_h_re, diag_h_im, coupling_re, coupling_im, inject_re, inject_im, dephasing, lead_slice, lead_slot):
    size_n = field_re.shape[0]
    bfield_re = field_re.astype(jnp.bfloat16)
    bfield_im = field_im.astype(jnp.bfloat16)
    wide_re = bfield_re.astype(jnp.float32)
    wide_im = bfield_im.astype(jnp.float32)
    zero_block = jnp.zeros((1, S, S), jnp.bfloat16)
    before_re = jnp.concatenate([zero_block, coupling_re[:-1]], axis=0)
    before_im = jnp.concatenate([zero_block, coupling_im[:-1]], axis=0)
    slab_re = wide_re.reshape(NSLICE, S, size_n)
    slab_im = wide_im.reshape(NSLICE, S, size_n)
    zero_slab = jnp.zeros((1, S, size_n), jnp.float32)
    upper_re = jnp.concatenate([zero_slab, slab_re[:-1]], axis=0)
    upper_im = jnp.concatenate([zero_slab, slab_im[:-1]], axis=0)
    lower_re = jnp.concatenate([slab_re[1:], zero_slab], axis=0)
    lower_im = jnp.concatenate([slab_im[1:], zero_slab], axis=0)
    term_a = block_left("sij,sjn->sin", before_re, before_im, upper_re, upper_im, False)
    term_b = block_left("sij,sjn->sin", diag_h_re, diag_h_im, slab_re, slab_im, False)
    term_c = block_left("sji,sjn->sin", coupling_re, coupling_im, lower_re, lower_im, True)
    left_re = (term_a[0] + term_b[0] + term_c[0]).reshape(size_n, size_n)
    left_im = (term_a[1] + term_b[1] + term_c[1]).reshape(size_n, size_n)
    strip_re = wide_re.reshape(size_n, NSLICE, S)
    strip_im = wide_im.reshape(size_n, NSLICE, S)
    zero_strip = jnp.zeros((size_n, 1, S), jnp.float32)
    prior_re = jnp.concatenate([zero_strip, strip_re[:, :-1]], axis=1)
    prior_im = jnp.concatenate([zero_strip, strip_im[:, :-1]], axis=1)
    later_re = jnp.concatenate([strip_re[:, 1:], zero_strip], axis=1)
    later_im = jnp.concatenate([strip_im[:, 1:], zero_strip], axis=1)
    term_d = block_right("nsj,skj->nsk", prior_re, prior_im, before_re, before_im, True)
    term_e = block_right("nsj,sjk->nsk", strip_re, strip_im, diag_h_re, diag_h_im, False)
    term_f = block_right("nsj,sjk->nsk", later_re, later_im, coupling_re, coupling_im, False)
    right_re = (term_d[0] + term_e[0] + term_f[0]).reshape(size_n, size_n)
    right_im = (term_d[1] + term_e[1] + term_f[1]).reshape(size_n, size_n)
    comm_re = left_re - right_re
    comm_im = left_im - right_im
    global_index = lax.iota(jnp.int32, size_n)
    off_diag = (global_index[:, None] != global_index[None, :]).astype(jnp.float32)
    rate = 0.5 * (dephasing[:, None] + dephasing[None, :]) * off_diag
    gen_re = comm_im - rate * field_re
    gen_im = -comm_re - rate * field_im
    for lead_index in range(LEADS):
        place = lead_slice[lead_index].astype(jnp.int32)
        slot_index = lead_slot[lead_index].astype(jnp.int32)
        kblock_re = lax.dynamic_index_in_dim(inject_re, slot_index, 0, keepdims=False).astype(jnp.float32)
        kblock_im = lax.dynamic_index_in_dim(inject_im, slot_index, 0, keepdims=False).astype(jnp.float32)
        start_cell = (place * S).astype(jnp.int32)
        rows_re = lax.dynamic_slice_in_dim(wide_re, start_cell, S, 0)
        rows_im = lax.dynamic_slice_in_dim(wide_im, start_cell, S, 0)
        made_re = jnp.dot(kblock_re, rows_re) - jnp.dot(kblock_im, rows_im)
        made_im = jnp.dot(kblock_re, rows_im) + jnp.dot(kblock_im, rows_re)
        gen_re = lax.dynamic_update_slice_in_dim(gen_re, lax.dynamic_slice_in_dim(gen_re, start_cell, S, 0) - made_re, start_cell, 0)
        gen_im = lax.dynamic_update_slice_in_dim(gen_im, lax.dynamic_slice_in_dim(gen_im, start_cell, S, 0) - made_im, start_cell, 0)
        cols_re = lax.dynamic_slice_in_dim(wide_re, start_cell, S, 1)
        cols_im = lax.dynamic_slice_in_dim(wide_im, start_cell, S, 1)
        side_re = jnp.dot(cols_re, kblock_re.T) + jnp.dot(cols_im, kblock_im.T)
        side_im = jnp.dot(cols_im, kblock_re.T) - jnp.dot(cols_re, kblock_im.T)
        gen_re = lax.dynamic_update_slice_in_dim(gen_re, lax.dynamic_slice_in_dim(gen_re, start_cell, S, 1) - side_re, start_cell, 1)
        gen_im = lax.dynamic_update_slice_in_dim(gen_im, lax.dynamic_slice_in_dim(gen_im, start_cell, S, 1) - side_im, start_cell, 1)
    return step_scale * gen_re, step_scale * gen_im


def reference(rho_re, rho_im, diag_re, diag_im, coupling_re, coupling_im, inject_re, inject_im, dephasing, lead_slice, lead_slot):
    diag_h_re, diag_h_im = hermitian(diag_re, diag_im)
    one_re, one_im = generator(rho_re, rho_im, diag_h_re, diag_h_im, coupling_re, coupling_im, inject_re, inject_im, dephasing, lead_slice, lead_slot)
    next_re, next_im = generator(one_re, one_im, diag_h_re, diag_h_im, coupling_re, coupling_im, inject_re, inject_im, dephasing, lead_slice, lead_slot)
    two_re = 2.0 * next_re - rho_re
    two_im = 2.0 * next_im - rho_im
    prop_re = coeff_zero * rho_re + coeff_one * one_re + coeff_two * two_re
    prop_im = coeff_zero * rho_im + coeff_one * one_im + coeff_two * two_im
    return prop_re, prop_im
```

```python
import jax
import jax.numpy as jnp
from jax import lax
from jax.experimental import pallas as pl
from jax.experimental.pallas import tpu as pltpu
from jax.sharding import PartitionSpec as P

S = 256
LEADS = 4
PIECE = 16

step_scale = 0.25
coeff_zero = 0.7652
coeff_one = 0.8801
coeff_two = 0.2298

BF = jnp.bfloat16
F32 = jnp.float32
MESH = pl.DeviceIdType.MESH


def nn(a, b):
    return jnp.dot(a, b, preferred_element_type=F32)


def nt(a, b):
    return lax.dot_general(a, b, (((1,), (1,)), ((), ())), preferred_element_type=F32)


def pick(key, table):
    out = jnp.int32(table[-1])
    for i in range(len(table) - 1):
        out = jnp.where(key == i, jnp.int32(table[i]), out)
    return out


STEP_OF = ((1, 0, 2, 4, 4, 4, 4, 3), (3, 1, 4, 4, 4, 4, 2, 0))
OFF_OF = ((1, 0, 2, 7), (7, 1, 6, 0))


def kernel(
    rho_re, rho_im, diag_re, diag_im, coup_re, coup_im, inj_re, inj_im, deph,
    lead_slice, lead_slot,
    out_re, out_im,
    field, part, far, right, q_out, q_in, kmine, kall, dmat, lpiece, lcol, lrow, crow, cprev,
    l_part, l_far, rate, phi,
    y_send, y_recv, z_send, z_recv, c_send, c_recv, q_send, q_recv,
    k_send, k_recv, a_send, a_recv, b_send, b_recv, h_send, h_recv, s_send, s_recv,
):
    r = lax.axis_index("row")
    c = lax.axis_index("col")
    core = c % 2
    y_lo = r % 2
    partner = r + 1 - 2 * y_lo
    relay = (r + 2 - 4 * y_lo + 16) % 16
    relay_from = (r - 2 + 4 * y_lo + 16) % 16
    c_next = (c + 1) % 16
    c_prior = (c + 15) % 16
    c_mate = c + 1 - 2 * core

    def dev(a, b):
        return {"row": a, "col": b}

    zr, xc, hc = r // 2, (c // 2) % 4, c // 8
    sources = []
    for j in range(2):
        q = (r + 16 - j) % 16
        step = (xc + 4 - (q // 2) % 4) % 4
        zp = (zr + pick(step, OFF_OF[j])) % 8
        yp = jnp.where(hc == q // 8, y_lo, 1 - y_lo)
        sources.append((2 * zp + yp, q))
    targets = []
    for j in range(2):
        row_to = (c + j) % 16
        step = pick((r // 2 + 8 - row_to // 2) % 8, STEP_OF[j])
        x_to = ((c // 2) % 4 + step) % 4
        h_to = jnp.where(y_lo == row_to % 2, c // 8, 1 - c // 8)
        targets.append((step < 4, row_to, 8 * h_to + 2 * x_to))

    barrier = pltpu.get_barrier_semaphore()

    def greet(a, b):
        pl.semaphore_signal(barrier, inc=1, device_id=dev(a, b), device_id_type=MESH)

    greet(partner, c)
    greet(relay_from, c)
    greet(r, c_next)
    greet(r, c_prior)
    greet(r, c_mate)
    for p, q in sources:
        greet(p, q)

    @pl.loop(1, 16)
    def _(i):
        greet(r, (c + i) % 16)
        greet((r + i) % 16, c)

    @pl.loop(0, 16)
    def _(i):
        @pl.when(jnp.logical_or(i != r, c != r))
        def _():
            greet(i, r)

    field[0] = rho_re[...].astype(BF)
    field[1] = rho_im[...].astype(BF)
    rows16 = pl.ds(pl.multiple_of(r * PIECE, PIECE), PIECE)
    kmine[0] = inj_re[0, rows16, :]
    kmine[1] = inj_im[0, rows16, :]
    kall[c] = kmine[...]

    own_piece = jnp.where(r == c, 1, 0)
    sends_h = sum(jnp.where(t[0], 2, 0) for t in targets)
    pl.semaphore_wait(barrier, 5 + 30 + 16 - own_piece + sends_h)

    def remote(src, dst, ss, rs, to):
        return pltpu.make_async_remote_copy(
            src_ref=src, dst_ref=dst, send_sem=ss, recv_sem=rs, device_id=to, device_id_type=MESH
        )

    def row_copies(g):
        ys = [remote(field.at[2 * g + i], part.at[2 * g + i], y_send.at[2 * g + i], y_recv.at[2 * g + i], dev(partner, c)) for i in range(2)]
        zs = [remote(part.at[2 * g + i], far.at[2 * g + i], z_send.at[2 * g + i], z_recv.at[2 * g + i], dev(relay, c)) for i in range(2)]
        return ys, zs

    def col_copies(g):
        two = pl.ds(2 * g, 2)
        cs = remote(field.at[two], right.at[two], c_send.at[g], c_recv.at[g], dev(r, c_prior))
        qs = remote(q_out.at[two], q_in.at[two], q_send.at[g], q_recv.at[g], dev(r, c_next))
        return cs, qs

    ys, zs = row_copies(0)
    for y in ys:
        y.start()

    @pl.loop(1, 16)
    def _(i):
        remote(kmine, kall.at[c], k_send, k_recv, dev(r, (c + i) % 16)).start()

    cs, qs = col_copies(0)
    cs.start()
    for j, (on, row_to, col_to) in enumerate(targets):
        land = (crow, cprev)[j]

        @pl.when(on)
        def _():
            remote(coup_re.at[0], land.at[0], h_send.at[2 * j], h_recv.at[j], dev(row_to, col_to)).start()
            remote(coup_im.at[0], land.at[1], h_send.at[2 * j + 1], h_recv.at[j], dev(row_to, col_to + 1)).start()

    def product_right(g):
        fr, fi = field[2 * g], field[2 * g + 1]
        cr, ci = coup_re[0], coup_im[0]
        q_out[2 * g] = (nt(fr, ci) - nt(fi, cr)).astype(BF)
        q_out[2 * g + 1] = (nt(fr, cr) + nt(fi, ci)).astype(BF)

    product_right(0)
    qs.start()

    gr = diag_re[0].astype(F32)
    gi = diag_im[0].astype(F32)
    dmat[0] = (0.5 * (gr + gr.T)).astype(BF)
    dmat[1] = (0.5 * (gi - gi.T)).astype(BF)

    g_rows = deph[pl.ds(pl.multiple_of(r * S, S), S)].reshape(1, S)
    g_cols = deph[pl.ds(pl.multiple_of(c * S, S), S)].reshape(1, S)
    wide = jnp.broadcast_to(g_rows, (S, S)).T + jnp.broadcast_to(g_cols, (S, S))
    ii = lax.broadcasted_iota(jnp.int32, (S, S), 0) + r * S
    jj = lax.broadcasted_iota(jnp.int32, (S, S), 1) + c * S
    rate[...] = jnp.where(ii == jj, 0.0, 0.5 * wide)

    def drain(ref, sem):
        pltpu.make_async_copy(ref, ref, sem).wait()

    drain(kall.at[pl.ds(0, 15)], k_recv)
    sum_re = dmat[1, rows16, :].astype(F32)
    sum_im = -dmat[0, rows16, :].astype(F32)
    for l in range(LEADS):
        block = kall[lead_slot[l]].astype(F32)
        hit = jnp.where(lead_slice[l] == c, 1.0, 0.0)
        sum_re = sum_re - hit * block[0]
        sum_im = sum_im - hit * block[1]
    lpiece[0] = sum_re.astype(BF)
    lpiece[1] = sum_im.astype(BF)
    lcol[r] = lpiece[...]

    @pl.loop(0, 16)
    def _(i):
        @pl.when(jnp.logical_or(r != c, i != c))
        def _():
            remote(lpiece.at[i % 2], lrow.at[i % 2, r], b_send, b_recv, dev(c, i)).start()

    @pl.when(r == c)
    def _():
        lrow[core, r] = lpiece[core]

    @pl.loop(1, 16)
    def _(i):
        remote(lpiece, lcol.at[r], a_send, a_recv, dev((r + i) % 16, c)).start()

    for y, z in zip(ys, zs):
        y.wait_recv()
        z.start()

    shares = []
    for j, land in enumerate((crow, cprev)):
        pltpu.make_async_copy(land.at[0], land.at[0], h_recv.at[j]).wait()
        s = remote(land.at[core], land.at[core], s_send.at[j], s_recv.at[j], dev(r, c_mate))
        s.start()
        shares.append(s)

    @pl.when(r == c)
    def _():
        drain(lrow.at[0, pl.ds(0, 15)], b_recv)

    @pl.when(r != c)
    def _():
        drain(lrow.at[0], b_recv)

    s = remote(lrow.at[core], lrow.at[core], s_send.at[2], s_recv.at[2], dev(r, c_mate))
    s.start()
    shares.append(s)

    shares[0].wait_recv()
    shares[1].wait_recv()
    has_prior = jnp.where(r > 0, 1.0, 0.0).astype(BF)
    minus_prior = jnp.where(r > 0, -1.0, 0.0).astype(BF)
    minus_next = jnp.where(r < 15, -1.0, 0.0).astype(BF)

    def place(to_prior, to_next):
        to_prior[0] = has_prior * cprev[1]
        to_prior[1] = minus_prior * cprev[0]
        to_next[0] = minus_next * crow[1].T
        to_next[1] = minus_next * crow[0].T

    @pl.when(y_lo == 0)
    def _():
        place(l_far, l_part)

    @pl.when(y_lo == 1)
    def _():
        place(l_part, l_far)

    shares[2].wait_recv()
    drain(lcol.at[pl.ds(0, 15)], a_recv)

    def left_add(acc, lr, li, fr, fi):
        return (acc[0] + nn(lr, fr) - nn(li, fi), acc[1] + nn(lr, fi) + nn(li, fr))

    not_last = jnp.where(c < 15, 1.0, 0.0)
    not_first = jnp.where(c > 0, 1.0, 0.0)

    def generator(g, own_re, own_im, zs, cs, qs):
        fr, fi = field[2 * g], field[2 * g + 1]
        acc = (-rate[...] * own_re, -rate[...] * own_im)
        acc = left_add(acc, lrow[0].reshape(S, S), lrow[1].reshape(S, S), fr, fi)
        kr, ki = lcol[:, 0].reshape(S, S), lcol[:, 1].reshape(S, S)
        acc = (acc[0] + nt(fr, kr) + nt(fi, ki), acc[1] + nt(fi, kr) - nt(fr, ki))
        acc = left_add(acc, l_part[0], l_part[1], part[2 * g], part[2 * g + 1])
        cs.wait_recv()
        nr, ni = right[2 * g], right[2 * g + 1]
        cr, ci = coup_re[0], coup_im[0]
        acc = (
            acc[0] - not_last * (nn(nr, ci) + nn(ni, cr)),
            acc[1] + not_last * (nn(nr, cr) - nn(ni, ci)),
        )
        qs.wait_recv()
        acc = (
            acc[0] + not_first * q_in[2 * g].astype(F32),
            acc[1] + not_first * q_in[2 * g + 1].astype(F32),
        )
        for z in zs:
            z.wait_recv()
        acc = left_add(acc, l_far[0], l_far[1], far[2 * g], far[2 * g + 1])
        return step_scale * acc[0], step_scale * acc[1]

    one_re, one_im = generator(0, rho_re[...], rho_im[...], zs, cs, qs)
    field[2] = one_re.astype(BF)
    field[3] = one_im.astype(BF)
    ys2, zs2 = row_copies(1)
    cs2, qs2 = col_copies(1)
    for y in ys2:
        y.start()
    cs2.start()
    phi[0] = one_re
    phi[1] = one_im
    product_right(1)
    qs2.start()
    for y, z in zip(ys2, zs2):
        y.wait_recv()
        z.start()
    two_re, two_im = generator(1, phi[0], phi[1], zs2, cs2, qs2)
    out_re[...] = (coeff_zero - coeff_two) * rho_re[...] + coeff_one * phi[0] + 2.0 * coeff_two * two_re
    out_im[...] = (coeff_zero - coeff_two) * rho_im[...] + coeff_one * phi[1] + 2.0 * coeff_two * two_im

    for copies in (ys, zs, ys2, zs2, (cs, cs2, qs, qs2), shares):
        for one in copies:
            one.wait_send()
    drain(kall.at[pl.ds(0, 15)], k_send)
    drain(lcol.at[pl.ds(0, 15)], a_send)

    @pl.when(r == c)
    def _():
        drain(lrow.at[0, pl.ds(0, 15)], b_send)

    @pl.when(r != c)
    def _():
        drain(lrow.at[0], b_send)

    for j, (on, row_to, col_to) in enumerate(targets):
        @pl.when(on)
        def _():
            pltpu.make_async_copy(coup_re.at[0], coup_re.at[0], h_send.at[2 * j]).wait()
            pltpu.make_async_copy(coup_im.at[0], coup_im.at[0], h_send.at[2 * j + 1]).wait()


def shards(*args):
    vm = pl.BlockSpec(memory_space=pltpu.VMEM)
    sm = pl.BlockSpec(memory_space=pltpu.SMEM)
    dma = pltpu.SemaphoreType.DMA

    def blocks(n):
        return pltpu.VMEM((n, S, S), BF)

    pieces = (16, 2, PIECE, S)
    return pl.pallas_call(
        kernel,
        name="propagate",
        out_shape=[jax.ShapeDtypeStruct((S, S), F32)] * 2,
        in_specs=[vm] * 9 + [sm] * 2,
        out_specs=[vm] * 2,
        scratch_shapes=[
            blocks(4), blocks(4), blocks(4), blocks(4), blocks(4), blocks(4),
            pltpu.VMEM((2, PIECE, S), BF), pltpu.VMEM(pieces, BF), blocks(2),
            pltpu.VMEM((2, PIECE, S), BF), pltpu.VMEM(pieces, BF), pltpu.VMEM((2, 16, PIECE, S), BF),
            blocks(2), blocks(2), blocks(2), blocks(2),
            pltpu.VMEM((S, S), F32), pltpu.VMEM((2, S, S), F32),
            dma((4,)), dma((4,)), dma((4,)), dma((4,)), dma((2,)), dma((2,)), dma((2,)), dma((2,)),
            dma, dma, dma, dma, dma, dma, dma((4,)), dma((2,)), dma((3,)), dma((3,)),
        ],
        compiler_params=pltpu.CompilerParams(
            collective_id=0, has_side_effects=True, vmem_limit_bytes=32 << 20
        ),
    )(*args)


def solution(mesh):
    return jax.shard_map(
        shards,
        mesh=mesh,
        in_specs=(
            P("row", "col"), P("row", "col"),
            P("col", None, None), P("col", None, None), P("col", None, None), P("col", None, None),
            P("col", None, None), P("col", None, None),
            P(), P(), P(),
        ),
        out_specs=(P("row", "col"), P("row", "col")),
        check_vma=False,
    )
```

```python
import jax
import jax.numpy as jnp
from jax import lax
from jax.experimental import pallas as pl
from jax.experimental.pallas import tpu as pltpu
from jax.sharding import PartitionSpec as P

S = 256
LEADS = 4
PIECE = 16

step_scale = 0.25
coeff_zero = 0.7652
coeff_one = 0.8801
coeff_two = 0.2298

BF = jnp.bfloat16
F32 = jnp.float32
MESH = pl.DeviceIdType.MESH


def nn(a, b):
    return jnp.dot(a, b, preferred_element_type=F32)


def nt(a, b):
    return lax.dot_general(a, b, (((1,), (1,)), ((), ())), preferred_element_type=F32)


def pick(key, table):
    out = jnp.int32(table[-1])
    for i in range(len(table) - 1):
        out = jnp.where(key == i, jnp.int32(table[i]), out)
    return out


STEP_OF = ((1, 0, 2, 4, 4, 4, 4, 3), (3, 1, 4, 4, 4, 4, 2, 0))
OFF_OF = ((1, 0, 2, 7), (7, 1, 6, 0))

HALF = 128


def kernel(
    rho_re_hbm, rho_im_hbm, diag_re_hbm, diag_im_hbm, coup_re_hbm, coup_im_hbm, inj_re_hbm, inj_im_hbm,
    deph_hbm, lead_slice_hbm, lead_slot_hbm,
    out_re_hbm, out_im_hbm,
    rho, diag, coup, deph, lead_slice, lead_slot, result,
    field, part, far, own, right, q_out, q_in,
    kmine, kall, dmat, lpiece, kcol, lrow, crow, cprev, l_part, l_far, rate, acc, phi, fix,
    in_sem, out_sem,
    y_send, y_recv, z_send, z_recv, c_send, c_recv, q_send, q_recv,
    k_send, k_recv, ay_send, ay_recv, a_send, a_recv, b_send, b_recv, h_send, h_recv, s_send, s_recv,
):
    r = lax.axis_index("row")
    c = lax.axis_index("col")
    core = c % 2
    y_lo = r % 2
    partner = r + 1 - 2 * y_lo
    relay = (r + 2 - 4 * y_lo + 16) % 16
    c_mate = c + 1 - 2 * core
    c_out = c - 1 + 2 * core
    has_out = jnp.logical_and(c_out >= 0, c_out < 16)

    def dev(a, b):
        return {"row": a, "col": b}

    def local(src, dst, i):
        return pltpu.make_async_copy(src, dst, in_sem.at[i])

    rows16 = pl.ds(pl.multiple_of(r * PIECE, PIECE), PIECE)
    loads = [
        local(inj_re_hbm.at[0, rows16, :], kmine.at[0], 0),
        local(inj_im_hbm.at[0, rows16, :], kmine.at[1], 1),
        local(rho_re_hbm, rho.at[0], 2),
        local(rho_im_hbm, rho.at[1], 3),
        local(coup_re_hbm.at[0], coup.at[0], 4),
        local(coup_im_hbm.at[0], coup.at[1], 5),
        local(diag_re_hbm.at[0], diag.at[0], 6),
        local(diag_im_hbm.at[0], diag.at[1], 7),
        local(deph_hbm, deph, 8),
        local(lead_slice_hbm, lead_slice, 9),
        local(lead_slot_hbm, lead_slot, 10),
    ]
    for load in loads:
        load.start()

    zr, xc, hc = r // 2, (c // 2) % 4, c // 8
    sources = []
    for j in range(2):
        q = (r + 16 - j) % 16
        step = (xc + 4 - (q // 2) % 4) % 4
        zp = (zr + pick(step, OFF_OF[j])) % 8
        yp = jnp.where(hc == q // 8, y_lo, 1 - y_lo)
        sources.append((2 * zp + yp, q))
    targets = []
    for j in range(2):
        row_to = (c + j) % 16
        step = pick((r // 2 + 8 - row_to // 2) % 8, STEP_OF[j])
        x_to = ((c // 2) % 4 + step) % 4
        h_to = jnp.where(y_lo == row_to % 2, c // 8, 1 - c // 8)
        targets.append((step < 4, row_to, 8 * h_to + 2 * x_to))

    barrier = pltpu.get_barrier_semaphore()

    def greet(a, b):
        pl.semaphore_signal(barrier, inc=1, device_id=dev(a, b), device_id_type=MESH)

    @pl.loop(0, 16)
    def _(i):
        @pl.when(jnp.logical_or(i != r, c != r))
        def _():
            greet(i, r)

    for p, q in sources:
        greet(p, q)

    @pl.loop(1, 8)
    def _(i):
        greet(r, (c + 2 * i) % 16)
        greet((r + 2 * i) % 16, c)

    @pl.when(has_out)
    def _():
        greet(r, c_out)

    greet(partner, c)
    greet(r, c_mate)

    for load in loads[:4]:
        load.wait()
    kslot = 8 * core + c // 2
    kall[kslot] = kmine[...]

    def halves(ref, value_re, value_im):
        for p, value in enumerate((value_re, value_im)):
            for h in range(2):
                ref[h, p] = value[:, h * HALF : (h + 1) * HALF]

    halves(field.at[0], rho[0].astype(BF), rho[1].astype(BF))

    @pl.when(c == 15)
    def _():
        right[...] = jnp.zeros_like(right)

    @pl.when(c == 0)
    def _():
        q_in[...] = jnp.zeros_like(q_in)

    own_piece = jnp.where(r == c, 1, 0)
    sends_h = sum(jnp.where(t[0], 2, 0) for t in targets)
    pl.semaphore_wait(barrier, 2 + jnp.where(has_out, 1, 0) + 14 + 16 - own_piece + sends_h)

    def remote(src, dst, ss, rs, to):
        return pltpu.make_async_remote_copy(
            src_ref=src, dst_ref=dst, send_sem=ss, recv_sem=rs, device_id=to, device_id_type=MESH
        )

    def drain(ref, sem):
        pltpu.make_async_copy(ref, ref, sem).wait()

    def row_copies(g):
        ys, zs = [], []
        for h in range(2):
            for p in range(2):
                i = 4 * g + 2 * h + p
                ys.append(remote(field.at[g, h, p], part.at[g, h, p], y_send.at[i], y_recv.at[i], dev(partner, c)))
                zs.append(remote(part.at[g, h, p], far.at[g, h, p], z_send.at[i], z_recv.at[i], dev(relay, c)))
        return ys, zs

    def col_copies(g, src):
        cs = remote(src, right.at[g], c_send.at[g], c_recv.at[g], dev(r, c - 1))
        qs = remote(q_out.at[g], q_in.at[g], q_send.at[g], q_recv.at[g], dev(r, c + 1))
        return cs, qs

    def full(ref):
        return (
            jnp.concatenate([ref[0, 0], ref[1, 0]], axis=1),
            jnp.concatenate([ref[0, 1], ref[1, 1]], axis=1),
        )

    @pl.loop(1, 8)
    def _(i):
        remote(kmine, kall.at[kslot], k_send, k_recv, dev(r, (c + 2 * i) % 16)).start()

    ys, zs = row_copies(0)
    for y in ys:
        y.start()
    cs, qs = col_copies(0, field.at[0])

    @pl.when(c > 0)
    def _():
        cs.start()

    for load in loads[4:]:
        load.wait()

    for j, (on, row_to, col_to) in enumerate(targets):
        land = (crow, cprev)[j]

        @pl.when(on)
        def _():
            remote(coup.at[0], land.at[0], h_send.at[2 * j], h_recv.at[j], dev(row_to, col_to)).start()
            remote(coup.at[1], land.at[1], h_send.at[2 * j + 1], h_recv.at[j], dev(row_to, col_to + 1)).start()

    def product_right(g, fr, fi):
        cr, ci = coup[0], coup[1]
        q_out[g, 0] = (nt(fr, ci) - nt(fi, cr)).astype(BF)
        q_out[g, 1] = (nt(fr, cr) + nt(fi, ci)).astype(BF)

    fr, fi = full(field.at[0])
    product_right(0, fr, fi)

    @pl.when(c < 15)
    def _():
        qs.start()

    gr = diag[0].astype(F32)
    gi = diag[1].astype(F32)
    dmat[0] = (0.5 * (gr + gr.T)).astype(BF)
    dmat[1] = (0.5 * (gi - gi.T)).astype(BF)

    def forward(y, z):
        y.wait_recv()
        z.start()

    forward(ys[0], zs[0])
    drain(kall.at[pl.ds(0, 7)], k_recv)
    eight = pl.ds(8 * core, 8)
    swap = remote(kall.at[eight], kall.at[eight], s_send.at[3], s_recv.at[3], dev(r, c_mate))
    swap.start()
    forward(ys[1], zs[1])

    g_rows = deph[pl.ds(pl.multiple_of(r * S, S), S)].reshape(1, S)
    g_cols = deph[pl.ds(pl.multiple_of(c * S, S), S)].reshape(1, S)
    wide = jnp.broadcast_to(g_rows, (S, S)).T + jnp.broadcast_to(g_cols, (S, S))
    ii = lax.broadcasted_iota(jnp.int32, (S, S), 0) + r * S
    jj = lax.broadcasted_iota(jnp.int32, (S, S), 1) + c * S
    rate[...] = jnp.where(ii == jj, 0.0, 0.5 * wide)

    swap.wait_recv()
    sum_re = jnp.zeros((PIECE, S), F32)
    sum_im = jnp.zeros((PIECE, S), F32)
    for l in range(LEADS):
        slot = lead_slot[l]
        block = kall[8 * (slot % 2) + slot // 2].astype(F32)
        hit = jnp.where(lead_slice[l] == c, 1.0, 0.0)
        sum_re = sum_re + hit * block[0]
        sum_im = sum_im + hit * block[1]
    lpiece[0] = (dmat[1, rows16, :].astype(F32) - sum_re).astype(BF)
    lpiece[1] = (-dmat[0, rows16, :].astype(F32) - sum_im).astype(BF)
    kcol[r, 0] = sum_re.astype(BF)
    kcol[r, 1] = sum_im.astype(BF)

    @pl.loop(0, 16)
    def _(i):
        @pl.when(jnp.logical_or(r != c, i != c))
        def _():
            remote(lpiece.at[i % 2], lrow.at[i % 2, r], b_send, b_recv, dev(c, i)).start()

    @pl.when(r == c)
    def _():
        lrow[core, r] = lpiece[core]

    ay = remote(kcol.at[r], kcol.at[r], ay_send, ay_recv, dev(partner, c))
    ay.start()
    forward(ys[2], zs[2])
    forward(ys[3], zs[3])

    ay.wait_recv()
    pair = pl.ds(r - y_lo, 2)

    @pl.loop(1, 8)
    def _(i):
        remote(kcol.at[pair], kcol.at[pair], a_send, a_recv, dev((r + 2 * i) % 16, c)).start()

    def local_terms(own_re, own_im, fr, fi):
        dr, di = dmat[0], dmat[1]
        acc[0] = -rate[...] * own_re - nn(fr, di) - nn(fi, dr)
        acc[1] = -rate[...] * own_im + nn(fr, dr) - nn(fi, di)

    local_terms(rho[0], rho[1], fr, fi)

    shares = []
    for j, land in enumerate((crow, cprev)):
        pltpu.make_async_copy(land.at[0], land.at[0], h_recv.at[j]).wait()
        s = remote(land.at[core], land.at[core], s_send.at[j], s_recv.at[j], dev(r, c_mate))
        s.start()
        shares.append(s)

    def add_right(g):
        @pl.when(c < 15)
        def _():
            cs.wait_recv()

        nr, ni = full(right.at[g])
        cr, ci = coup[0], coup[1]
        acc[0] -= nn(nr, ci) + nn(ni, cr)
        acc[1] += nn(nr, cr) - nn(ni, ci)

    def add_q(g):
        @pl.when(c > 0)
        def _():
            qs.wait_recv()

        acc[0] += q_in[g, 0].astype(F32)
        acc[1] += q_in[g, 1].astype(F32)

    add_right(0)
    add_q(0)

    shares[0].wait_recv()
    shares[1].wait_recv()
    has_prior = jnp.where(r > 0, 1.0, 0.0).astype(BF)
    minus_prior = jnp.where(r > 0, -1.0, 0.0).astype(BF)
    minus_next = jnp.where(r < 15, -1.0, 0.0).astype(BF)

    def place(to_prior, to_next):
        to_prior[0] = has_prior * cprev[1]
        to_prior[1] = minus_prior * cprev[0]
        to_next[0] = minus_next * crow[1].T
        to_next[1] = minus_next * crow[0].T

    @pl.when(y_lo == 0)
    def _():
        place(l_far, l_part)

    @pl.when(y_lo == 1)
    def _():
        place(l_part, l_far)

    def left(lr, li, fr, fi):
        return nn(lr, fr) - nn(li, fi), nn(lr, fi) + nn(li, fr)

    def add_left(h, lr, li, fr, fi):
        more = left(lr, li, fr, fi)
        span = slice(h * HALF, (h + 1) * HALF)
        acc[0, :, span] += more[0]
        acc[1, :, span] += more[1]

    for h in range(2):
        add_left(h, l_part[0], l_part[1], part[0, h, 0], part[0, h, 1])

    @pl.when(r == c)
    def _():
        drain(lrow.at[0, pl.ds(0, 15)], b_recv)

    @pl.when(r != c)
    def _():
        drain(lrow.at[0], b_recv)

    s = remote(lrow.at[core], lrow.at[core], s_send.at[2], s_recv.at[2], dev(r, c_mate))
    s.start()
    shares.append(s)
    s.wait_recv()
    lr, li = lrow[0].reshape(S, S), lrow[1].reshape(S, S)
    more = left(lr, li, fr, fi)
    acc[0] += more[0]
    acc[1] += more[1]

    ys2, zs2 = row_copies(1)
    for h in range(2):
        zs[2 * h].wait_recv()
        zs[2 * h + 1].wait_recv()
        more = left(l_far[0], l_far[1], far[0, h, 0], far[0, h, 1])
        span = slice(h * HALF, (h + 1) * HALF)
        for p in range(2):
            value = step_scale * (acc[p, :, span] + more[p])
            phi[p, :, span] = value
            field[1, h, p] = value.astype(BF)
            ys2[2 * h + p].start()

    drain(kcol.at[pl.ds(0, 14)], a_recv)

    def lead_right(fr, fi):
        kr, ki = kcol[:, 0].reshape(S, S), kcol[:, 1].reshape(S, S)
        return step_scale * (nt(fr, kr) + nt(fi, ki)), step_scale * (nt(fi, kr) - nt(fr, ki))

    less = lead_right(fr, fi)
    phi[0] = phi[0] - less[0]
    phi[1] = phi[1] - less[1]
    halves(own, phi[0].astype(BF), phi[1].astype(BF))
    cs0, qs0 = cs, qs
    cs, qs = col_copies(1, own)

    @pl.when(c > 0)
    def _():
        cs.start()

    gr, gi = full(own)
    product_right(1, gr, gi)

    @pl.when(c < 15)
    def _():
        qs.start()

    fix[0], fix[1] = lead_right(*full(part.at[0]))
    forward(ys2[0], zs2[0])
    fix[2], fix[3] = lead_right(*full(far.at[0]))
    forward(ys2[1], zs2[1])
    local_terms(phi[0], phi[1], gr, gi)
    less = lead_right(gr, gi)
    more = left(lr, li, gr, gi)
    for p in range(2):
        acc[p] += more[p] - less[p] * (1.0 / step_scale)
    forward(ys2[2], zs2[2])
    forward(ys2[3], zs2[3])

    def corrected(ref, k, h):
        span = slice(h * HALF, (h + 1) * HALF)
        return [(ref[1, h, p].astype(F32) - fix[k + p, :, span]).astype(BF) for p in range(2)]

    @pl.when(c < 15)
    def _():
        cs.wait_recv()

    nr, ni = full(right.at[1])
    cr, ci = coup[0], coup[1]
    acc[0] -= nn(nr, ci) + nn(ni, cr)
    acc[1] += nn(nr, cr) - nn(ni, ci)

    @pl.when(c > 0)
    def _():
        qs.wait_recv()

    for p in range(2):
        acc[p] += q_in[1, p].astype(F32)
    for h in range(2):
        add_left(h, l_part[0], l_part[1], *corrected(part, 0, h))
    for p in range(2):
        acc[p] = (
            (coeff_zero - coeff_two) * rho[p] + coeff_one * phi[p] + (2.0 * coeff_two * step_scale) * acc[p]
        )
    stores = []
    for h in range(2):
        zs2[2 * h].wait_recv()
        zs2[2 * h + 1].wait_recv()
        more = left(l_far[0], l_far[1], *corrected(far, 2, h))
        span = slice(h * HALF, (h + 1) * HALF)
        for p in range(2):
            result[p, :, span] = acc[p, :, span] + (2.0 * coeff_two * step_scale) * more[p]
            out = (out_re_hbm, out_im_hbm)[p]
            store = pltpu.make_async_copy(result.at[p, :, pl.ds(h * HALF, HALF)], out.at[:, pl.ds(h * HALF, HALF)], out_sem.at[2 * h + p])
            store.start()
            stores.append(store)

    for copies in (ys, zs, ys2, zs2, shares, (swap, ay)):
        for one in copies:
            one.wait_send()

    @pl.when(c > 0)
    def _():
        cs0.wait_send()
        cs.wait_send()

    @pl.when(c < 15)
    def _():
        qs0.wait_send()
        qs.wait_send()

    drain(kall.at[pl.ds(0, 7)], k_send)
    drain(kcol.at[pl.ds(0, 14)], a_send)

    @pl.when(r == c)
    def _():
        drain(lrow.at[0, pl.ds(0, 15)], b_send)

    @pl.when(r != c)
    def _():
        drain(lrow.at[0], b_send)

    for j, (on, row_to, col_to) in enumerate(targets):
        @pl.when(on)
        def _():
            pltpu.make_async_copy(coup.at[0], coup.at[0], h_send.at[2 * j]).wait()
            pltpu.make_async_copy(coup.at[1], coup.at[1], h_send.at[2 * j + 1]).wait()

    for store in stores:
        store.wait()


def shards(*args):
    hbm = pl.BlockSpec(memory_space=pl.ANY)
    dma = pltpu.SemaphoreType.DMA

    def blocks(*n):
        return pltpu.VMEM((*n, S, S), BF)

    def split(*n):
        return pltpu.VMEM((*n, 2, 2, S, HALF), BF)

    pieces = (16, 2, PIECE, S)
    return pl.pallas_call(
        kernel,
        name="propagate",
        out_shape=[jax.ShapeDtypeStruct((S, S), F32)] * 2,
        in_specs=[hbm] * 11,
        out_specs=[hbm] * 2,
        scratch_shapes=[
            pltpu.VMEM((2, S, S), F32), blocks(2), blocks(2), pltpu.VMEM((16 * S,), F32),
            pltpu.SMEM((LEADS,), jnp.int32), pltpu.SMEM((LEADS,), jnp.int32), pltpu.VMEM((2, S, S), F32),
            split(2), split(2), split(2), split(), split(2), blocks(2, 2), blocks(2, 2),
            pltpu.VMEM((2, PIECE, S), BF), pltpu.VMEM(pieces, BF), blocks(2),
            pltpu.VMEM((2, PIECE, S), BF), pltpu.VMEM(pieces, BF), pltpu.VMEM((2, 16, PIECE, S), BF),
            blocks(2), blocks(2), blocks(2), blocks(2),
            pltpu.VMEM((S, S), F32), pltpu.VMEM((2, S, S), F32), pltpu.VMEM((2, S, S), F32), pltpu.VMEM((4, S, S), F32),
            dma((11,)), dma((4,)),
            dma((8,)), dma((8,)), dma((8,)), dma((8,)), dma((2,)), dma((2,)), dma((2,)), dma((2,)),
            dma, dma, dma, dma, dma, dma, dma, dma, dma((4,)), dma((2,)), dma((4,)), dma((4,)),
        ],
        compiler_params=pltpu.CompilerParams(
            collective_id=0, has_side_effects=True, vmem_limit_bytes=60 << 20
        ),
    )(*args)


def solution(mesh):
    return jax.shard_map(
        shards,
        mesh=mesh,
        in_specs=(
            P("row", "col"), P("row", "col"),
            P("col", None, None), P("col", None, None), P("col", None, None), P("col", None, None),
            P("col", None, None), P("col", None, None),
            P(), P(), P(),
        ),
        out_specs=(P("row", "col"), P("row", "col")),
        check_vma=False,
    )
```

```python
import jax
import jax.numpy as jnp
from jax import lax
from jax.experimental import pallas as pl
from jax.experimental.pallas import tpu as pltpu
from jax.sharding import PartitionSpec as P

S = 256
LEADS = 4
PIECE = 16

step_scale = 0.25
coeff_zero = 0.7652
coeff_one = 0.8801
coeff_two = 0.2298

BF = jnp.bfloat16
F32 = jnp.float32
MESH = pl.DeviceIdType.MESH


def nn(a, b):
    return jnp.dot(a, b, preferred_element_type=F32)


def nt(a, b):
    return lax.dot_general(a, b, (((1,), (1,)), ((), ())), preferred_element_type=F32)


HALF = 128


def kernel(
    rho_re_hbm, rho_im_hbm, diag_re_hbm, diag_im_hbm, coup_re_hbm, coup_im_hbm, inj_re_hbm, inj_im_hbm,
    deph_hbm, lead_slice_hbm, lead_slot_hbm,
    out_re_hbm, out_im_hbm,
    rho, diag, coup, inj, deph, lead_slice, lead_slot, result,
    field, part, far, own, right, q_out, q_in,
    kmine, kall, dmat, kcol, msum, m_in, rs_in, y_sum, y_in, lrow, crow, cprev, l_part, l_far, rate, acc, phi, fix,
    in_sem, out_sem,
    y_send, y_recv, z_send, z_recv, c_send, c_recv, q_send, q_recv,
    k_send, k_recv, ay_send, ay_recv, a_send, a_recv, h_send, h_recv, s_send, s_recv,
    m_send, m_recv, rs_send, rs_recv, hi_send, hi_recv, ag_send, ag_recv,
):
    r = lax.axis_index("row")
    c = lax.axis_index("col")
    core = c % 2
    y_lo = r % 2
    partner = r + 1 - 2 * y_lo
    relay = (r + 2 - 4 * y_lo + 16) % 16
    c_mate = c + 1 - 2 * core
    c_out = c - 1 + 2 * core
    has_out = jnp.logical_and(c_out >= 0, c_out < 16)

    def dev(a, b):
        return {"row": a, "col": b}

    def local(src, dst, i):
        return pltpu.make_async_copy(src, dst, in_sem.at[i])

    rows16 = pl.ds(pl.multiple_of(r * PIECE, PIECE), PIECE)
    loads = [
        local(inj_re_hbm.at[0, rows16, :], kmine.at[0], 0),
        local(inj_im_hbm.at[0, rows16, :], kmine.at[1], 1),
        local(rho_re_hbm, rho.at[0], 2),
        local(rho_im_hbm, rho.at[1], 3),
        local(coup_re_hbm.at[0], coup.at[0], 4),
        local(coup_im_hbm.at[0], coup.at[1], 5),
        local(diag_re_hbm.at[0], diag.at[0], 6),
        local(diag_im_hbm.at[0], diag.at[1], 7),
        local(deph_hbm, deph, 8),
        local(lead_slice_hbm, lead_slice, 9),
        local(lead_slot_hbm, lead_slot, 10),
        local(inj_re_hbm.at[0], inj.at[0], 11),
        local(inj_im_hbm.at[0], inj.at[1], 12),
    ]
    for load in loads:
        load.start()

    z, x, hi = r // 2, (c // 2) % 4, c // 8
    way = 1 - 2 * core

    def col(hi, x, core):
        return 8 * hi + 2 * ((x + 8) % 4) + core

    z_side = (z + 8 + 1 - 2 * y_lo) % 8
    rings = []
    for j in range(2):
        q = (r + 16 - j) % 16
        dist = ((x - (q // 2) % 4) * way + 8) % 4
        near = hi == q // 8
        start_far = jnp.where(core == 0, r + 1 - 2 * y_lo, 2 * z_side + 1 - y_lo)
        rings.append(dict(
            q=q,
            enters=jnp.logical_and(dist == 0, jnp.logical_not(near)),
            first=jnp.logical_and(dist == 1, near),
            start_far=start_far,
            passes=jnp.logical_and(dist < 3, jnp.logical_or(dist > 0, jnp.logical_not(near))),
        ))
    roots = []
    for j in range(2):
        to = (c + j) % 16
        to_lo = to % 2
        other = (to // 2 + 8 + 1 - 2 * to_lo) % 8
        roots.append(dict(
            to=to,
            own=r == to,
            far_re=r == to + 1 - 2 * to_lo,
            far_im=r == 2 * other + 1 - to_lo,
        ))

    barrier = pltpu.get_barrier_semaphore()

    def greet(a, b):
        pl.semaphore_signal(barrier, inc=1, device_id=dev(a, b), device_id_type=MESH)

    for ring in rings:
        @pl.when(ring["enters"])
        def _():
            greet(ring["start_far"], ring["q"])

        @pl.when(ring["first"])
        def _():
            greet(r, ring["q"])

    @pl.loop(1, 8)
    def _(i):
        greet(r, (c + 2 * i) % 16)
        greet((r + 2 * i) % 16, c)

    @pl.when(has_out)
    def _():
        greet(r, c_out)

    greet(partner, c)
    greet(r, c_mate)

    for load in loads[:4]:
        load.wait()
    kslot = 8 * core + c // 2
    kall[kslot] = kmine[...]

    def halves(ref, value_re, value_im):
        for p, value in enumerate((value_re, value_im)):
            for h in range(2):
                ref[h, p] = value[:, h * HALF : (h + 1) * HALF]

    halves(field.at[0], rho[0].astype(BF), rho[1].astype(BF))

    @pl.when(c == 15)
    def _():
        right[...] = jnp.zeros_like(right)

    @pl.when(c == 0)
    def _():
        q_in[...] = jnp.zeros_like(q_in)

    sends_h = sum(
        jnp.where(t["own"], 2, 0) + jnp.where(t["far_re"], 1, 0) + jnp.where(t["far_im"], 1, 0) for t in roots
    )
    pl.semaphore_wait(barrier, 2 + jnp.where(has_out, 1, 0) + 14 + sends_h)

    def remote(src, dst, ss, rs, to):
        return pltpu.make_async_remote_copy(
            src_ref=src, dst_ref=dst, send_sem=ss, recv_sem=rs, device_id=to, device_id_type=MESH
        )

    def drain(ref, sem):
        pltpu.make_async_copy(ref, ref, sem).wait()

    def row_copies(g):
        ys, zs = [], []
        for h in range(2):
            for p in range(2):
                i = 4 * g + 2 * h + p
                ys.append(remote(field.at[g, h, p], part.at[g, h, p], y_send.at[i], y_recv.at[i], dev(partner, c)))
                zs.append(remote(part.at[g, h, p], far.at[g, h, p], z_send.at[i], z_recv.at[i], dev(relay, c)))
        return ys, zs

    def col_copies(g, src):
        cs = remote(src, right.at[g], c_send.at[g], c_recv.at[g], dev(r, c - 1))
        qs = remote(q_out.at[g], q_in.at[g], q_send.at[g], q_recv.at[g], dev(r, c + 1))
        return cs, qs

    def full(ref):
        return (
            jnp.concatenate([ref[0, 0], ref[1, 0]], axis=1),
            jnp.concatenate([ref[0, 1], ref[1, 1]], axis=1),
        )

    ys, zs = row_copies(0)
    for y in ys:
        y.start()
    for load in loads[4:]:
        load.wait()

    gr = diag[0].astype(F32)
    gi = diag[1].astype(F32)
    dmat[0] = (0.5 * (gr + gr.T)).astype(BF)
    dmat[1] = (0.5 * (gi - gi.T)).astype(BF)

    mine = jnp.where(r == c, 1.0, 0.0)
    hits = jnp.float32(0.0)
    for l in range(LEADS):
        hits = hits + jnp.where(jnp.logical_and(lead_slice[l] == r, lead_slot[l] == c), 1.0, 0.0)
    share_re = mine * dmat[1].astype(F32) - hits * inj[0].astype(F32)
    share_im = -mine * dmat[0].astype(F32) - hits * inj[1].astype(F32)
    msum[0] = share_re.astype(BF).reshape(4, 64, S)
    msum[1] = share_im.astype(BF).reshape(4, 64, S)
    to_mate = remote(msum.at[1 - core], m_in, m_send, m_recv, dev(r, c_mate))
    to_mate.start()

    lands = (crow, cprev)
    h_copies = []
    for j, root in enumerate(roots):
        for u in range(2):
            rows = pl.ds(128 * u, 128)
            i = 2 * j + u

            def send(kind, on, p, to):
                copy = remote(coup.at[p, rows], lands[j].at[p, rows], h_send.at[6 * i + kind], h_recv.at[i], to)
                h_copies.append((on, copy))

                @pl.when(on)
                def _():
                    copy.start()

            to = root["to"]
            send(0, root["own"], 0, dev(to, col(hi, x + 1, 0)))
            send(1, root["own"], 1, dev(to, col(hi, x - 1, 1)))
            send(2, root["own"], 1 - core, dev(to, c_mate))
            send(3, root["far_re"], 0, dev(to, col(1 - hi, x, 0)))
            send(4, root["far_im"], 1, dev(to, col(1 - hi, x, 1)))

        @pl.when(root["own"])
        def _():
            lands[j][core] = coup[core]

    def pass_on(j, u):
        rows = pl.ds(128 * u, 128)
        i = 2 * j + u
        place = lands[j].at[core, rows]
        on = rings[j]["passes"]
        copy = remote(place, place, h_send.at[6 * i + 5], h_recv.at[i], dev(r, col(hi, x + way, core)))
        h_copies.append((on, copy))

        @pl.when(on)
        def _():
            copy.wait_recv()
            copy.start()

    @pl.loop(1, 8)
    def _(i):
        remote(kmine, kall.at[kslot], k_send, k_recv, dev(r, (c + 2 * i) % 16)).start()

    cs, qs = col_copies(0, field.at[0])

    @pl.when(c > 0)
    def _():
        cs.start()

    to_mate.wait_recv()
    msum[core] = (msum[core].astype(F32) + m_in[...].astype(F32)).astype(BF)
    scatter, gather = [], []
    for i in range(1, 4):
        peer = dev(r, col(hi, x + i, core))
        scatter.append(remote(msum.at[core, (x + i) % 4], rs_in.at[i - 1], rs_send.at[i - 1], rs_recv.at[i - 1], peer))
        quarter = lrow.at[core, x]
        gather.append(remote(quarter, quarter, ag_send.at[i - 1], ag_recv.at[i - 1], peer))
    for copy in scatter:
        copy.start()

    def product_right(g, fr, fi):
        cr, ci = coup[0], coup[1]
        q_out[g, 0] = (nt(fr, ci) - nt(fi, cr)).astype(BF)
        q_out[g, 1] = (nt(fr, cr) + nt(fi, ci)).astype(BF)

    fr, fi = full(field.at[0])
    product_right(0, fr, fi)

    @pl.when(c < 15)
    def _():
        qs.start()

    def forward(y, z):
        y.wait_recv()
        z.start()

    forward(ys[0], zs[0])
    pass_on(0, 0)
    for copy in scatter:
        copy.wait_recv()
    total = msum[core, x].astype(F32)
    for i in range(3):
        total = total + rs_in[i].astype(F32)
    y_sum[...] = total.astype(BF)
    cross = remote(y_sum, y_in, hi_send, hi_recv, dev(r, (c + 8) % 16))
    cross.start()
    forward(ys[1], zs[1])
    pass_on(0, 1)

    g_rows = deph[pl.ds(pl.multiple_of(r * S, S), S)].reshape(1, S)
    g_cols = deph[pl.ds(pl.multiple_of(c * S, S), S)].reshape(1, S)
    wide = jnp.broadcast_to(g_rows, (S, S)).T + jnp.broadcast_to(g_cols, (S, S))
    ii = lax.broadcasted_iota(jnp.int32, (S, S), 0) + r * S
    jj = lax.broadcasted_iota(jnp.int32, (S, S), 1) + c * S
    rate[...] = jnp.where(ii == jj, 0.0, 0.5 * wide)

    drain(kall.at[pl.ds(0, 7)], k_recv)
    eight = pl.ds(8 * core, 8)
    swap = remote(kall.at[eight], kall.at[eight], s_send.at[3], s_recv.at[3], dev(r, c_mate))
    swap.start()
    forward(ys[2], zs[2])
    pass_on(1, 0)
    cross.wait_recv()
    lrow[core, x] = (y_sum[...].astype(F32) + y_in[...].astype(F32)).astype(BF)
    for copy in gather:
        copy.start()
    forward(ys[3], zs[3])
    pass_on(1, 1)

    swap.wait_recv()
    sum_re = jnp.zeros((PIECE, S), F32)
    sum_im = jnp.zeros((PIECE, S), F32)
    for l in range(LEADS):
        slot = lead_slot[l]
        block = kall[8 * (slot % 2) + slot // 2].astype(F32)
        hit = jnp.where(lead_slice[l] == c, 1.0, 0.0)
        sum_re = sum_re + hit * block[0]
        sum_im = sum_im + hit * block[1]
    kcol[r, 0] = sum_re.astype(BF)
    kcol[r, 1] = sum_im.astype(BF)
    ay = remote(kcol.at[r], kcol.at[r], ay_send, ay_recv, dev(partner, c))
    ay.start()

    def local_terms(own_re, own_im, fr, fi):
        dr, di = dmat[0], dmat[1]
        acc[0] = -rate[...] * own_re - nn(fr, di) - nn(fi, dr)
        acc[1] = -rate[...] * own_im + nn(fr, dr) - nn(fi, di)

    local_terms(rho[0], rho[1], fr, fi)

    shares = []
    for j, land in enumerate(lands):
        for u in range(2):
            @pl.when(jnp.logical_and(c != rings[j]["q"], jnp.logical_not(rings[j]["passes"])))
            def _():
                part_of = land.at[0, pl.ds(128 * u, 128)]
                pltpu.make_async_copy(part_of, part_of, h_recv.at[2 * j + u]).wait()

        share = remote(land.at[core], land.at[core], s_send.at[j], s_recv.at[j], dev(r, c_mate))
        share.start()
        shares.append(share)

    ay.wait_recv()
    pair = pl.ds(r - y_lo, 2)

    @pl.loop(1, 8)
    def _(i):
        remote(kcol.at[pair], kcol.at[pair], a_send, a_recv, dev((r + 2 * i) % 16, c)).start()

    for copy in gather:
        copy.wait_recv()
    share = remote(lrow.at[core], lrow.at[core], s_send.at[2], s_recv.at[2], dev(r, c_mate))
    share.start()
    shares.append(share)

    def add_right(g):
        @pl.when(c < 15)
        def _():
            cs.wait_recv()

        nr, ni = full(right.at[g])
        cr, ci = coup[0], coup[1]
        acc[0] -= nn(nr, ci) + nn(ni, cr)
        acc[1] += nn(nr, cr) - nn(ni, ci)

    def add_q(g):
        @pl.when(c > 0)
        def _():
            qs.wait_recv()

        acc[0] += q_in[g, 0].astype(F32)
        acc[1] += q_in[g, 1].astype(F32)

    add_right(0)
    add_q(0)

    shares[0].wait_recv()
    shares[1].wait_recv()
    has_prior = jnp.where(r > 0, 1.0, 0.0).astype(BF)
    minus_prior = jnp.where(r > 0, -1.0, 0.0).astype(BF)
    minus_next = jnp.where(r < 15, -1.0, 0.0).astype(BF)

    def place(to_prior, to_next):
        to_prior[0] = has_prior * cprev[1]
        to_prior[1] = minus_prior * cprev[0]
        to_next[0] = minus_next * crow[1].T
        to_next[1] = minus_next * crow[0].T

    @pl.when(y_lo == 0)
    def _():
        place(l_far, l_part)

    @pl.when(y_lo == 1)
    def _():
        place(l_part, l_far)

    def left(lr, li, fr, fi):
        return nn(lr, fr) - nn(li, fi), nn(lr, fi) + nn(li, fr)

    def add_left(h, lr, li, fr, fi):
        more = left(lr, li, fr, fi)
        span = slice(h * HALF, (h + 1) * HALF)
        acc[0, :, span] += more[0]
        acc[1, :, span] += more[1]

    for h in range(2):
        add_left(h, l_part[0], l_part[1], part[0, h, 0], part[0, h, 1])

    shares[2].wait_recv()
    lr, li = lrow[0].reshape(S, S), lrow[1].reshape(S, S)
    more = left(lr, li, fr, fi)
    acc[0] += more[0]
    acc[1] += more[1]

    ys2, zs2 = row_copies(1)
    for h in range(2):
        zs[2 * h].wait_recv()
        zs[2 * h + 1].wait_recv()
        more = left(l_far[0], l_far[1], far[0, h, 0], far[0, h, 1])
        span = slice(h * HALF, (h + 1) * HALF)
        for p in range(2):
            value = step_scale * (acc[p, :, span] + more[p])
            phi[p, :, span] = value
            field[1, h, p] = value.astype(BF)
            ys2[2 * h + p].start()

    drain(kcol.at[pl.ds(0, 14)], a_recv)

    def lead_right(fr, fi):
        kr, ki = kcol[:, 0].reshape(S, S), kcol[:, 1].reshape(S, S)
        return step_scale * (nt(fr, kr) + nt(fi, ki)), step_scale * (nt(fi, kr) - nt(fr, ki))

    less = lead_right(fr, fi)
    phi[0] = phi[0] - less[0]
    phi[1] = phi[1] - less[1]
    halves(own, phi[0].astype(BF), phi[1].astype(BF))
    cs0, qs0 = cs, qs
    cs, qs = col_copies(1, own)

    @pl.when(c > 0)
    def _():
        cs.start()

    gr, gi = full(own)
    product_right(1, gr, gi)

    @pl.when(c < 15)
    def _():
        qs.start()

    fix[0], fix[1] = lead_right(*full(part.at[0]))
    forward(ys2[0], zs2[0])
    fix[2], fix[3] = lead_right(*full(far.at[0]))
    forward(ys2[1], zs2[1])
    local_terms(phi[0], phi[1], gr, gi)
    less = lead_right(gr, gi)
    more = left(lr, li, gr, gi)
    for p in range(2):
        acc[p] += more[p] - less[p] * (1.0 / step_scale)
    forward(ys2[2], zs2[2])
    forward(ys2[3], zs2[3])

    def corrected(ref, k, h):
        span = slice(h * HALF, (h + 1) * HALF)
        return [(ref[1, h, p].astype(F32) - fix[k + p, :, span]).astype(BF) for p in range(2)]

    @pl.when(c < 15)
    def _():
        cs.wait_recv()

    nr, ni = full(right.at[1])
    cr, ci = coup[0], coup[1]
    acc[0] -= nn(nr, ci) + nn(ni, cr)
    acc[1] += nn(nr, cr) - nn(ni, ci)

    @pl.when(c > 0)
    def _():
        qs.wait_recv()

    for p in range(2):
        acc[p] += q_in[1, p].astype(F32)
    for h in range(2):
        add_left(h, l_part[0], l_part[1], *corrected(part, 0, h))
    for p in range(2):
        acc[p] = (
            (coeff_zero - coeff_two) * rho[p] + coeff_one * phi[p] + (2.0 * coeff_two * step_scale) * acc[p]
        )
    stores = []
    for h in range(2):
        zs2[2 * h].wait_recv()
        zs2[2 * h + 1].wait_recv()
        more = left(l_far[0], l_far[1], *corrected(far, 2, h))
        span = slice(h * HALF, (h + 1) * HALF)
        for p in range(2):
            result[p, :, span] = acc[p, :, span] + (2.0 * coeff_two * step_scale) * more[p]
            out = (out_re_hbm, out_im_hbm)[p]
            store = pltpu.make_async_copy(result.at[p, :, pl.ds(h * HALF, HALF)], out.at[:, pl.ds(h * HALF, HALF)], out_sem.at[2 * h + p])
            store.start()
            stores.append(store)

    for copies in (ys, zs, ys2, zs2, shares, scatter, gather, (swap, ay, to_mate, cross)):
        for one in copies:
            one.wait_send()

    @pl.when(c > 0)
    def _():
        cs0.wait_send()
        cs.wait_send()

    @pl.when(c < 15)
    def _():
        qs0.wait_send()
        qs.wait_send()

    drain(kall.at[pl.ds(0, 7)], k_send)
    drain(kcol.at[pl.ds(0, 14)], a_send)

    for on, copy in h_copies:
        @pl.when(on)
        def _():
            copy.wait_send()

    for store in stores:
        store.wait()


def shards(*args):
    hbm = pl.BlockSpec(memory_space=pl.ANY)
    dma = pltpu.SemaphoreType.DMA

    def blocks(*n):
        return pltpu.VMEM((*n, S, S), BF)

    def split(*n):
        return pltpu.VMEM((*n, 2, 2, S, HALF), BF)

    def quarters(*n):
        return pltpu.VMEM((*n, 64, S), BF)

    pieces = (16, 2, PIECE, S)
    return pl.pallas_call(
        kernel,
        name="propagate",
        out_shape=[jax.ShapeDtypeStruct((S, S), F32)] * 2,
        in_specs=[hbm] * 11,
        out_specs=[hbm] * 2,
        scratch_shapes=[
            pltpu.VMEM((2, S, S), F32), blocks(2), blocks(2), blocks(2), pltpu.VMEM((16 * S,), F32),
            pltpu.SMEM((LEADS,), jnp.int32), pltpu.SMEM((LEADS,), jnp.int32), pltpu.VMEM((2, S, S), F32),
            split(2), split(2), split(2), split(), split(2), blocks(2, 2), blocks(2, 2),
            pltpu.VMEM((2, PIECE, S), BF), pltpu.VMEM(pieces, BF), blocks(2),
            pltpu.VMEM(pieces, BF), quarters(2, 4), quarters(4), quarters(3), quarters(), quarters(), quarters(2, 4),
            blocks(2), blocks(2), blocks(2), blocks(2),
            pltpu.VMEM((S, S), F32), pltpu.VMEM((2, S, S), F32), pltpu.VMEM((2, S, S), F32), pltpu.VMEM((4, S, S), F32),
            dma((13,)), dma((4,)),
            dma((8,)), dma((8,)), dma((8,)), dma((8,)), dma((2,)), dma((2,)), dma((2,)), dma((2,)),
            dma, dma, dma, dma, dma, dma, dma((24,)), dma((4,)), dma((4,)), dma((4,)),
            dma, dma, dma((3,)), dma((3,)), dma, dma, dma((3,)), dma((3,)),
        ],
        compiler_params=pltpu.CompilerParams(
            collective_id=0, has_side_effects=True, vmem_limit_bytes=60 << 20
        ),
    )(*args)


def solution(mesh):
    return jax.shard_map(
        shards,
        mesh=mesh,
        in_specs=(
            P("row", "col"), P("row", "col"),
            P("col", None, None), P("col", None, None), P("col", None, None), P("col", None, None),
            P("col", None, None), P("col", None, None),
            P(), P(), P(),
        ),
        out_specs=(P("row", "col"), P("row", "col")),
        check_vma=False,
    )
```

```python
import jax
import jax.numpy as jnp
from jax import lax
from jax.experimental import pallas as pl
from jax.experimental.pallas import tpu as pltpu
from jax.sharding import PartitionSpec as P

S = 256
LEADS = 4
PIECE = 16

step_scale = 0.25
coeff_zero = 0.7652
coeff_one = 0.8801
coeff_two = 0.2298

BF = jnp.bfloat16
F32 = jnp.float32
MESH = pl.DeviceIdType.MESH


def nn(a, b):
    return jnp.dot(a, b, preferred_element_type=F32)


def nt(a, b):
    return lax.dot_general(a, b, (((1,), (1,)), ((), ())), preferred_element_type=F32)


HALF = 128


def kernel(
    rho_re_hbm, rho_im_hbm, diag_re_hbm, diag_im_hbm, coup_re_hbm, coup_im_hbm, inj_re_hbm, inj_im_hbm,
    deph_hbm, lead_slice_hbm, lead_slot_hbm,
    out_re, out_im,
    rho, diag, coup, inj, deph, lead_slice, lead_slot,
    field, part, far, own, right, q_out, q_in,
    kmine, kall, dmat, kcol, msum, m_in, rs_in, y_sum, y_in, lrow, crow, cprev, l_part, l_far, rate, acc, phi, fix,
    in_sem,
    y_send, y_recv, z_send, z_recv, c_send, c_recv, q_send, q_recv,
    k_send, k_recv, ay_send, ay_recv, a_send, a_recv, h_send, h_recv, s_send, s_recv,
    m_send, m_recv, rs_send, rs_recv, hi_send, hi_recv, ag_send, ag_recv,
):
    r = lax.axis_index("row")
    c = lax.axis_index("col")
    core = c % 2
    y_lo = r % 2
    partner = r + 1 - 2 * y_lo
    relay = (r + 2 - 4 * y_lo + 16) % 16
    c_mate = c + 1 - 2 * core
    c_out = c - 1 + 2 * core
    has_out = jnp.logical_and(c_out >= 0, c_out < 16)

    def dev(a, b):
        return {"row": a, "col": b}

    def local(src, dst, i):
        return pltpu.make_async_copy(src, dst, in_sem.at[i])

    rows16 = pl.ds(pl.multiple_of(r * PIECE, PIECE), PIECE)
    loads = [
        local(inj_re_hbm.at[0, rows16, :], kmine.at[0], 0),
        local(inj_im_hbm.at[0, rows16, :], kmine.at[1], 1),
        local(rho_re_hbm, rho.at[0], 2),
        local(rho_im_hbm, rho.at[1], 3),
        local(coup_re_hbm.at[0], coup.at[0], 4),
        local(coup_im_hbm.at[0], coup.at[1], 5),
        local(diag_re_hbm.at[0], diag.at[0], 6),
        local(diag_im_hbm.at[0], diag.at[1], 7),
        local(deph_hbm, deph, 8),
        local(lead_slice_hbm, lead_slice, 9),
        local(lead_slot_hbm, lead_slot, 10),
        local(inj_re_hbm.at[0], inj.at[0], 11),
        local(inj_im_hbm.at[0], inj.at[1], 12),
    ]
    for load in loads:
        load.start()

    z, x, hi = r // 2, (c // 2) % 4, c // 8
    way = 1 - 2 * core

    def col(hi, x, core):
        return 8 * hi + 2 * ((x + 8) % 4) + core

    z_side = (z + 8 + 1 - 2 * y_lo) % 8
    rings = []
    for j in range(2):
        q = (r + 16 - j) % 16
        dist = ((x - (q // 2) % 4) * way + 8) % 4
        near = hi == q // 8
        start_far = jnp.where(core == 0, r + 1 - 2 * y_lo, 2 * z_side + 1 - y_lo)
        rings.append(dict(
            q=q,
            enters=jnp.logical_and(dist == 0, jnp.logical_not(near)),
            level=dist + jnp.where(near, 0, 1),
            first=jnp.logical_and(dist == 1, near),
            start_far=start_far,
            passes=jnp.logical_and(dist < 3, jnp.logical_or(dist > 0, jnp.logical_not(near))),
        ))
    roots = []
    for j in range(2):
        to = (c + j) % 16
        to_lo = to % 2
        other = (to // 2 + 8 + 1 - 2 * to_lo) % 8
        roots.append(dict(
            to=to,
            own=r == to,
            far_re=r == to + 1 - 2 * to_lo,
            far_im=r == 2 * other + 1 - to_lo,
        ))

    barrier = pltpu.get_barrier_semaphore()

    def greet(a, b):
        pl.semaphore_signal(barrier, inc=1, device_id=dev(a, b), device_id_type=MESH)

    for ring in rings:
        @pl.when(ring["enters"])
        def _():
            greet(ring["start_far"], ring["q"])

        @pl.when(ring["first"])
        def _():
            greet(r, ring["q"])

    @pl.loop(1, 8)
    def _(i):
        greet(r, (c + 2 * i) % 16)
        greet((r + 2 * i) % 16, c)

    @pl.when(has_out)
    def _():
        greet(r, c_out)

    greet(partner, c)
    greet(r, c_mate)

    for load in loads[:4]:
        load.wait()
    kslot = 8 * core + c // 2
    kall[kslot] = kmine[...]

    def halves(ref, value_re, value_im):
        for p, value in enumerate((value_re, value_im)):
            for h in range(2):
                ref[h, p] = value[:, h * HALF : (h + 1) * HALF]

    halves(field.at[0], rho[0].astype(BF), rho[1].astype(BF))

    @pl.when(c == 15)
    def _():
        right[...] = jnp.zeros_like(right)

    @pl.when(c == 0)
    def _():
        q_in[...] = jnp.zeros_like(q_in)

    sends_h = sum(
        jnp.where(t["own"], 2, 0) + jnp.where(t["far_re"], 1, 0) + jnp.where(t["far_im"], 1, 0) for t in roots
    )
    pl.semaphore_wait(barrier, 2 + jnp.where(has_out, 1, 0) + 14 + sends_h)

    def remote(src, dst, ss, rs, to):
        return pltpu.make_async_remote_copy(
            src_ref=src, dst_ref=dst, send_sem=ss, recv_sem=rs, device_id=to, device_id_type=MESH
        )

    def drain(ref, sem):
        pltpu.make_async_copy(ref, ref, sem).wait()

    def row_copies(g):
        ys, zs = [], []
        for h in range(2):
            for p in range(2):
                i = 4 * g + 2 * h + p
                ys.append(remote(field.at[g, h, p], part.at[g, h, p], y_send.at[i], y_recv.at[i], dev(partner, c)))
                zs.append(remote(part.at[g, h, p], far.at[g, h, p], z_send.at[i], z_recv.at[i], dev(relay, c)))
        return ys, zs

    def col_copies(g, src):
        cs = remote(src, right.at[g], c_send.at[g], c_recv.at[g], dev(r, c - 1))
        qs = remote(q_out.at[g], q_in.at[g], q_send.at[g], q_recv.at[g], dev(r, c + 1))
        return cs, qs

    def full(ref):
        return (
            jnp.concatenate([ref[0, 0], ref[1, 0]], axis=1),
            jnp.concatenate([ref[0, 1], ref[1, 1]], axis=1),
        )

    @pl.loop(1, 8)
    def _(i):
        remote(kmine, kall.at[kslot], k_send, k_recv, dev(r, (c + 2 * i) % 16)).start()

    ys, zs = row_copies(0)
    ys[0].start()
    ys[1].start()
    for load in loads[4:]:
        load.wait()

    gr = diag[0].astype(F32)
    gi = diag[1].astype(F32)
    dmat[0] = (0.5 * (gr + gr.T)).astype(BF)
    dmat[1] = (0.5 * (gi - gi.T)).astype(BF)

    mine = jnp.where(r == c, 1.0, 0.0)
    hits = jnp.float32(0.0)
    for l in range(LEADS):
        hits = hits + jnp.where(jnp.logical_and(lead_slice[l] == r, lead_slot[l] == c), 1.0, 0.0)
    share_re = mine * dmat[1].astype(F32) - hits * inj[0].astype(F32)
    share_im = -mine * dmat[0].astype(F32) - hits * inj[1].astype(F32)
    msum[0] = share_re.astype(BF).reshape(4, 64, S)
    msum[1] = share_im.astype(BF).reshape(4, 64, S)
    to_mate = remote(msum.at[1 - core], m_in, m_send, m_recv, dev(r, c_mate))
    to_mate.start()

    cs, qs = col_copies(0, field.at[0])

    to_mate.wait_recv()
    msum[core] = (msum[core].astype(F32) + m_in[...].astype(F32)).astype(BF)
    scatter, gather = [], []
    for i in range(1, 4):
        peer = dev(r, col(hi, x + i, core))
        scatter.append(remote(msum.at[core, (x + i) % 4], rs_in.at[i - 1], rs_send.at[i - 1], rs_recv.at[i - 1], peer))
        quarter = lrow.at[core, x]
        gather.append(remote(quarter, quarter, ag_send.at[i - 1], ag_recv.at[i - 1], peer))
    for copy in scatter:
        copy.start()

    lands = (crow, cprev)
    h_copies = []
    for j, root in enumerate(roots):
        for u in range(2):
            rows = pl.ds(128 * u, 128)
            i = 2 * j + u

            def send(kind, on, p, to):
                copy = remote(coup.at[p, rows], lands[j].at[p, rows], h_send.at[6 * i + kind], h_recv.at[i], to)
                h_copies.append((on, copy))

                @pl.when(on)
                def _():
                    copy.start()

            to = root["to"]
            send(0, root["own"], 0, dev(to, col(hi, x + 1, 0)))
            send(1, root["own"], 1, dev(to, col(hi, x - 1, 1)))
            send(2, root["own"], 1 - core, dev(to, c_mate))
            send(3, root["far_re"], 0, dev(to, col(1 - hi, x, 0)))
            send(4, root["far_im"], 1, dev(to, col(1 - hi, x, 1)))

        @pl.when(root["own"])
        def _():
            lands[j][core] = coup[core]

    onward = []
    for j in range(2):
        for u in range(2):
            i = 2 * j + u
            place = lands[j].at[core, pl.ds(128 * u, 128)]
            copy = remote(place, place, h_send.at[6 * i + 5], h_recv.at[i], dev(r, col(hi, x + way, core)))
            onward.append(copy)
            h_copies.append((rings[j]["passes"], copy))

    def pass_on(j, level):
        @pl.when(jnp.logical_and(rings[j]["passes"], rings[j]["level"] == level))
        def _():
            for copy in onward[2 * j : 2 * j + 2]:
                copy.wait_recv()
                copy.start()

    def product_right(g, fr, fi):
        cr, ci = coup[0], coup[1]
        q_out[g, 0] = (nt(fr, ci) - nt(fi, cr)).astype(BF)
        q_out[g, 1] = (nt(fr, cr) + nt(fi, ci)).astype(BF)

    fr, fi = full(field.at[0])
    product_right(0, fr, fi)

    def forward(y, z):
        y.wait_recv()
        z.start()

    def pieces_in():
        drain(kall.at[pl.ds(0, 7)], k_recv)
        swap.start()

    eight = pl.ds(8 * core, 8)
    swap = remote(kall.at[eight], kall.at[eight], s_send.at[3], s_recv.at[3], dev(r, c_mate))
    forward(ys[0], zs[0])
    ys[2].start()
    pieces_in()
    pass_on(0, 1)
    for copy in scatter:
        copy.wait_recv()
    total = msum[core, x].astype(F32)
    for i in range(3):
        total = total + rs_in[i].astype(F32)
    y_sum[...] = total.astype(BF)
    cross = remote(y_sum, y_in, hi_send, hi_recv, dev(r, (c + 8) % 16))
    cross.start()

    @pl.when(c > 0)
    def _():
        cs.start()

    @pl.when(c < 15)
    def _():
        qs.start()

    pass_on(1, 1)
    forward(ys[1], zs[1])
    ys[3].start()

    swap.wait_recv()
    sum_re = jnp.zeros((PIECE, S), F32)
    sum_im = jnp.zeros((PIECE, S), F32)
    for l in range(LEADS):
        slot = lead_slot[l]
        block = kall[8 * (slot % 2) + slot // 2].astype(F32)
        hit = jnp.where(lead_slice[l] == c, 1.0, 0.0)
        sum_re = sum_re + hit * block[0]
        sum_im = sum_im + hit * block[1]
    kcol[r, 0] = sum_re.astype(BF)
    kcol[r, 1] = sum_im.astype(BF)
    ay = remote(kcol.at[r], kcol.at[r], ay_send, ay_recv, dev(partner, c))
    ay.start()
    pass_on(0, 2)
    forward(ys[2], zs[2])
    pass_on(1, 2)
    ay.wait_recv()
    pair = pl.ds(r - y_lo, 2)

    @pl.loop(1, 8)
    def _(i):
        remote(kcol.at[pair], kcol.at[pair], a_send, a_recv, dev((r + 2 * i) % 16, c)).start()

    forward(ys[3], zs[3])
    cross.wait_recv()
    lrow[core, x] = (y_sum[...].astype(F32) + y_in[...].astype(F32)).astype(BF)
    for copy in gather:
        copy.start()

    pass_on(0, 3)
    pass_on(1, 3)

    g_rows = deph[pl.ds(pl.multiple_of(r * S, S), S)].reshape(1, S)
    g_cols = deph[pl.ds(pl.multiple_of(c * S, S), S)].reshape(1, S)
    wide = jnp.broadcast_to(g_rows, (S, S)).T + jnp.broadcast_to(g_cols, (S, S))
    ii = lax.broadcasted_iota(jnp.int32, (S, S), 0) + r * S
    jj = lax.broadcasted_iota(jnp.int32, (S, S), 1) + c * S
    rate[...] = jnp.where(ii == jj, 0.0, 0.5 * wide)

    def local_terms(own_re, own_im, fr, fi):
        dr, di = dmat[0], dmat[1]
        acc[0] = -rate[...] * own_re - nn(fr, di) - nn(fi, dr)
        acc[1] = -rate[...] * own_im + nn(fr, dr) - nn(fi, di)

    local_terms(rho[0], rho[1], fr, fi)

    shares = []
    for j, land in enumerate(lands):
        for u in range(2):
            @pl.when(jnp.logical_and(c != rings[j]["q"], jnp.logical_not(rings[j]["passes"])))
            def _():
                part_of = land.at[0, pl.ds(128 * u, 128)]
                pltpu.make_async_copy(part_of, part_of, h_recv.at[2 * j + u]).wait()

        share = remote(land.at[core], land.at[core], s_send.at[j], s_recv.at[j], dev(r, c_mate))
        share.start()
        shares.append(share)

    for copy in gather:
        copy.wait_recv()
    share = remote(lrow.at[core], lrow.at[core], s_send.at[2], s_recv.at[2], dev(r, c_mate))
    share.start()
    shares.append(share)

    def add_right(g):
        @pl.when(c < 15)
        def _():
            cs.wait_recv()

        nr, ni = full(right.at[g])
        cr, ci = coup[0], coup[1]
        acc[0] -= nn(nr, ci) + nn(ni, cr)
        acc[1] += nn(nr, cr) - nn(ni, ci)

    def add_q(g):
        @pl.when(c > 0)
        def _():
            qs.wait_recv()

        acc[0] += q_in[g, 0].astype(F32)
        acc[1] += q_in[g, 1].astype(F32)

    add_right(0)
    add_q(0)

    shares[0].wait_recv()
    shares[1].wait_recv()
    has_prior = jnp.where(r > 0, 1.0, 0.0).astype(BF)
    minus_prior = jnp.where(r > 0, -1.0, 0.0).astype(BF)
    minus_next = jnp.where(r < 15, -1.0, 0.0).astype(BF)

    def place(to_prior, to_next):
        to_prior[0] = has_prior * cprev[1]
        to_prior[1] = minus_prior * cprev[0]
        to_next[0] = minus_next * crow[1].T
        to_next[1] = minus_next * crow[0].T

    @pl.when(y_lo == 0)
    def _():
        place(l_far, l_part)

    @pl.when(y_lo == 1)
    def _():
        place(l_part, l_far)

    def left(lr, li, fr, fi):
        return nn(lr, fr) - nn(li, fi), nn(lr, fi) + nn(li, fr)

    def add_left(h, lr, li, fr, fi):
        more = left(lr, li, fr, fi)
        span = slice(h * HALF, (h + 1) * HALF)
        acc[0, :, span] += more[0]
        acc[1, :, span] += more[1]

    for h in range(2):
        add_left(h, l_part[0], l_part[1], part[0, h, 0], part[0, h, 1])

    shares[2].wait_recv()
    lr, li = lrow[0].reshape(S, S), lrow[1].reshape(S, S)
    more = left(lr, li, fr, fi)
    acc[0] += more[0]
    acc[1] += more[1]

    ys2, zs2 = row_copies(1)
    for h in range(2):
        zs[2 * h].wait_recv()
        zs[2 * h + 1].wait_recv()
        more = left(l_far[0], l_far[1], far[0, h, 0], far[0, h, 1])
        span = slice(h * HALF, (h + 1) * HALF)
        for p in range(2):
            value = step_scale * (acc[p, :, span] + more[p])
            phi[p, :, span] = value
            field[1, h, p] = value.astype(BF)
            ys2[2 * h + p].start()

    drain(kcol.at[pl.ds(0, 14)], a_recv)

    def lead_right(fr, fi):
        kr, ki = kcol[:, 0].reshape(S, S), kcol[:, 1].reshape(S, S)
        return step_scale * (nt(fr, kr) + nt(fi, ki)), step_scale * (nt(fi, kr) - nt(fr, ki))

    less = lead_right(fr, fi)
    phi[0] = phi[0] - less[0]
    phi[1] = phi[1] - less[1]
    halves(own, phi[0].astype(BF), phi[1].astype(BF))
    cs0, qs0 = cs, qs
    cs, qs = col_copies(1, own)

    @pl.when(c > 0)
    def _():
        cs.start()

    gr, gi = full(own)
    product_right(1, gr, gi)

    @pl.when(c < 15)
    def _():
        qs.start()

    fix[0], fix[1] = lead_right(*full(part.at[0]))
    forward(ys2[0], zs2[0])
    fix[2], fix[3] = lead_right(*full(far.at[0]))
    forward(ys2[1], zs2[1])
    local_terms(phi[0], phi[1], gr, gi)
    less = lead_right(gr, gi)
    more = left(lr, li, gr, gi)
    for p in range(2):
        acc[p] += more[p] - less[p] * (1.0 / step_scale)
    forward(ys2[2], zs2[2])
    forward(ys2[3], zs2[3])

    def corrected(ref, k, h):
        span = slice(h * HALF, (h + 1) * HALF)
        return [(ref[1, h, p].astype(F32) - fix[k + p, :, span]).astype(BF) for p in range(2)]

    @pl.when(c < 15)
    def _():
        cs.wait_recv()

    nr, ni = full(right.at[1])
    cr, ci = coup[0], coup[1]
    acc[0] -= nn(nr, ci) + nn(ni, cr)
    acc[1] += nn(nr, cr) - nn(ni, ci)

    @pl.when(c > 0)
    def _():
        qs.wait_recv()

    for p in range(2):
        acc[p] += q_in[1, p].astype(F32)
    for h in range(2):
        add_left(h, l_part[0], l_part[1], *corrected(part, 0, h))
    for p in range(2):
        acc[p] = (
            coeff_one * phi[p] + (2.0 * coeff_two * step_scale) * acc[p]
        )
    for h in range(2):
        zs2[2 * h].wait_recv()
        zs2[2 * h + 1].wait_recv()
        more = left(l_far[0], l_far[1], *corrected(far, 2, h))
        span = slice(h * HALF, (h + 1) * HALF)
        for p in range(2):
            out = (out_re, out_im)[p]
            out[:, span] = acc[p, :, span] + (2.0 * coeff_two * step_scale) * more[p]

    for copies in (ys, zs, ys2, zs2, shares, scatter, gather, (swap, ay, to_mate, cross)):
        for one in copies:
            one.wait_send()

    @pl.when(c > 0)
    def _():
        cs0.wait_send()
        cs.wait_send()

    @pl.when(c < 15)
    def _():
        qs0.wait_send()
        qs.wait_send()

    drain(kall.at[pl.ds(0, 7)], k_send)
    drain(kcol.at[pl.ds(0, 14)], a_send)

    for on, copy in h_copies:
        @pl.when(on)
        def _():
            copy.wait_send()


def shards(*args):
    hbm = pl.BlockSpec(memory_space=pl.ANY)
    dma = pltpu.SemaphoreType.DMA

    def blocks(*n):
        return pltpu.VMEM((*n, S, S), BF)

    def split(*n):
        return pltpu.VMEM((*n, 2, 2, S, HALF), BF)

    def quarters(*n):
        return pltpu.VMEM((*n, 64, S), BF)

    pieces = (16, 2, PIECE, S)
    outs = pl.pallas_call(
        kernel,
        name="propagate",
        out_shape=[jax.ShapeDtypeStruct((S, S), F32)] * 2,
        in_specs=[hbm] * 11,
        out_specs=[pl.BlockSpec(memory_space=pltpu.VMEM)] * 2,
        scratch_shapes=[
            pltpu.VMEM((2, S, S), F32), blocks(2), blocks(2), blocks(2), pltpu.VMEM((16 * S,), F32),
            pltpu.SMEM((LEADS,), jnp.int32), pltpu.SMEM((LEADS,), jnp.int32),
            split(2), split(2), split(2), split(), split(2), blocks(2, 2), blocks(2, 2),
            pltpu.VMEM((2, PIECE, S), BF), pltpu.VMEM(pieces, BF), blocks(2),
            pltpu.VMEM(pieces, BF), quarters(2, 4), quarters(4), quarters(3), quarters(), quarters(), quarters(2, 4),
            blocks(2), blocks(2), blocks(2), blocks(2),
            pltpu.VMEM((S, S), F32), pltpu.VMEM((2, S, S), F32), pltpu.VMEM((2, S, S), F32), pltpu.VMEM((4, S, S), F32),
            dma((13,)),
            dma((8,)), dma((8,)), dma((8,)), dma((8,)), dma((2,)), dma((2,)), dma((2,)), dma((2,)),
            dma, dma, dma, dma, dma, dma, dma((24,)), dma((4,)), dma((4,)), dma((4,)),
            dma, dma, dma((3,)), dma((3,)), dma, dma, dma((3,)), dma((3,)),
        ],
        compiler_params=pltpu.CompilerParams(
            collective_id=0, has_side_effects=True, vmem_limit_bytes=60 << 20
        ),
    )(*args)
    return tuple(o + (coeff_zero - coeff_two) * a for o, a in zip(outs, args))


def solution(mesh):
    return jax.shard_map(
        shards,
        mesh=mesh,
        in_specs=(
            P("row", "col"), P("row", "col"),
            P("col", None, None), P("col", None, None), P("col", None, None), P("col", None, None),
            P("col", None, None), P("col", None, None),
            P(), P(), P(),
        ),
        out_specs=(P("row", "col"), P("row", "col")),
        check_vma=False,
    )
```

```python
import jax
import jax.numpy as jnp
from jax import lax
from jax.experimental import pallas as pl
from jax.experimental.pallas import tpu as pltpu
from jax.sharding import PartitionSpec as P

S = 256
LEADS = 4
PIECE = 16

step_scale = 0.25
coeff_zero = 0.7652
coeff_one = 0.8801
coeff_two = 0.2298

BF = jnp.bfloat16
F32 = jnp.float32
MESH = pl.DeviceIdType.MESH


def nn(a, b):
    return jnp.dot(a, b, preferred_element_type=F32)


def nt(a, b):
    return lax.dot_general(a, b, (((1,), (1,)), ((), ())), preferred_element_type=F32)


HALF = 128


def kernel(
    rho_re_hbm, rho_im_hbm, diag_re_hbm, diag_im_hbm, coup_re_hbm, coup_im_hbm, inj_re_hbm, inj_im_hbm,
    deph_hbm, lead_slice_hbm, lead_slot_hbm,
    out_re, out_im,
    rho, diag, coup, inj, deph, lead_slice, lead_slot,
    field, part, far, own, right, q_out, q_in,
    kmine, kall, dmat, kcol, msum, m_in, rs_in, y_sum, y_in, lrow, crow, cprev, l_part, l_far, rate, acc, phi, fix,
    in_sem,
    y_send, y_recv, z_send, z_recv, c_send, c_recv, q_send, q_recv,
    k_send, k_recv, ay_send, ay_recv, a_send, a_recv, h_send, h_recv, s_send, s_recv,
    near_sem, far_sem, m_send, m_recv, rs_send, rs_recv, hi_send, hi_recv, ag_send, ag_recv,
):
    r = lax.axis_index("row")
    c = lax.axis_index("col")
    core = c % 2
    y_lo = r % 2
    partner = r + 1 - 2 * y_lo
    relay = (r + 2 - 4 * y_lo + 16) % 16
    c_mate = c + 1 - 2 * core
    c_out = c - 1 + 2 * core
    has_out = jnp.logical_and(c_out >= 0, c_out < 16)

    def dev(a, b):
        return {"row": a, "col": b}

    def local(src, dst, i):
        return pltpu.make_async_copy(src, dst, in_sem.at[i])

    rows16 = pl.ds(pl.multiple_of(r * PIECE, PIECE), PIECE)
    loads = [
        local(inj_re_hbm.at[0, rows16, :], kmine.at[0], 0),
        local(inj_im_hbm.at[0, rows16, :], kmine.at[1], 1),
        local(rho_re_hbm, rho.at[0], 2),
        local(rho_im_hbm, rho.at[1], 3),
        local(coup_re_hbm.at[0], coup.at[0], 4),
        local(coup_im_hbm.at[0], coup.at[1], 5),
        local(diag_re_hbm.at[0], diag.at[0], 6),
        local(diag_im_hbm.at[0], diag.at[1], 7),
        local(deph_hbm, deph, 8),
        local(lead_slice_hbm, lead_slice, 9),
        local(lead_slot_hbm, lead_slot, 10),
        local(inj_re_hbm.at[0], inj.at[0], 11),
        local(inj_im_hbm.at[0], inj.at[1], 12),
    ]
    for load in loads:
        load.start()

    z, x, hi = r // 2, (c // 2) % 4, c // 8
    way = 1 - 2 * core

    def col(hi, x, core):
        return 8 * hi + 2 * ((x + 8) % 4) + core

    def beside(z, y_lo):
        return jnp.where(y_lo == 0, jnp.where(z < 7, z + 1, 6), jnp.where(z > 0, z - 1, 1))

    z_side = beside(z, y_lo)
    gives_far = jnp.where(y_lo == 0, z, 7 - z) < 7
    gets_far = jnp.where(y_lo == 0, z, 7 - z) > 0
    rings = []
    for j in range(2):
        q = (r + 16 - j) % 16
        dist = ((x - (q // 2) % 4) * way + 8) % 4
        near = hi == q // 8
        start_far = jnp.where(core == 0, r + 1 - 2 * y_lo, 2 * z_side + 1 - y_lo)
        rings.append(dict(
            q=q,
            enters=jnp.logical_and(dist == 0, jnp.logical_not(near)),
            level=dist + jnp.where(near, 0, 1),
            first=jnp.logical_and(dist == 1, near),
            start_far=start_far,
            passes=jnp.logical_and(dist < 3, jnp.logical_or(dist > 0, jnp.logical_not(near))),
        ))
    roots = []
    for j in range(2):
        to = (c + j) % 16
        to_lo = to % 2
        other = beside(to // 2, to_lo)
        roots.append(dict(
            to=to,
            own=r == to,
            far_re=r == to + 1 - 2 * to_lo,
            far_im=r == 2 * other + 1 - to_lo,
        ))

    barrier = pltpu.get_barrier_semaphore()

    def greet(a, b):
        pl.semaphore_signal(barrier, inc=1, device_id=dev(a, b), device_id_type=MESH)

    for ring in rings:
        @pl.when(ring["enters"])
        def _():
            greet(ring["start_far"], ring["q"])

        @pl.when(ring["first"])
        def _():
            greet(r, ring["q"])

    @pl.loop(1, 8)
    def _(i):
        greet(r, (c + 2 * i) % 16)

        @pl.when(z + i < 8)
        def _():
            greet((r + 2 * i) % 16, c)

    @pl.when(has_out)
    def _():
        greet(r, c_out)

    greet(partner, c)
    greet(r, c_mate)

    for load in loads[:4]:
        load.wait()
    kslot = 8 * core + c // 2
    kall[kslot] = kmine[...]

    def halves(ref, value_re, value_im):
        for p, value in enumerate((value_re, value_im)):
            for h in range(2):
                ref[h, p] = value[:, h * HALF : (h + 1) * HALF]

    halves(field.at[0], rho[0].astype(BF), rho[1].astype(BF))

    @pl.when(c == 15)
    def _():
        right[...] = jnp.zeros_like(right)

    @pl.when(c == 0)
    def _():
        q_in[...] = jnp.zeros_like(q_in)

    @pl.when(jnp.logical_not(gets_far))
    def _():
        far[...] = jnp.zeros_like(far)

    sends_h = sum(
        jnp.where(t["own"], 2, 0) + jnp.where(t["far_re"], 1, 0) + jnp.where(t["far_im"], 1, 0) for t in roots
    )
    pl.semaphore_wait(barrier, 2 + jnp.where(has_out, 1, 0) + 7 + z + sends_h)

    def answer(sem, by):
        pl.semaphore_signal(sem, inc=1, device_id=dev((r + 16 - 2 * by) % 16, c), device_id_type=MESH)

    @pl.when(z > 0)
    def _():
        answer(near_sem, 1)

    @pl.loop(2, 8)
    def _(i):
        @pl.when(i <= z)
        def _():
            answer(far_sem, i)

    def remote(src, dst, ss, rs, to):
        return pltpu.make_async_remote_copy(
            src_ref=src, dst_ref=dst, send_sem=ss, recv_sem=rs, device_id=to, device_id_type=MESH
        )

    def drain(ref, sem):
        pltpu.make_async_copy(ref, ref, sem).wait()

    def row_copies(g):
        ys, zs = [], []
        for h in range(2):
            for p in range(2):
                i = 4 * g + 2 * h + p
                ys.append(remote(field.at[g, h, p], part.at[g, h, p], y_send.at[i], y_recv.at[i], dev(partner, c)))
                zs.append(remote(part.at[g, h, p], far.at[g, h, p], z_send.at[i], z_recv.at[i], dev(relay, c)))
        return ys, zs

    def col_copies(g, src):
        cs = remote(src, right.at[g], c_send.at[g], c_recv.at[g], dev(r, c - 1))
        qs = remote(q_out.at[g], q_in.at[g], q_send.at[g], q_recv.at[g], dev(r, c + 1))
        return cs, qs

    def full(ref):
        return (
            jnp.concatenate([ref[0, 0], ref[1, 0]], axis=1),
            jnp.concatenate([ref[0, 1], ref[1, 1]], axis=1),
        )

    @pl.loop(1, 8)
    def _(i):
        remote(kmine, kall.at[kslot], k_send, k_recv, dev(r, (c + 2 * i) % 16)).start()

    ys, zs = row_copies(0)
    ys[0].start()
    ys[1].start()
    for load in loads[4:]:
        load.wait()

    gr = diag[0].astype(F32)
    gi = diag[1].astype(F32)
    dmat[0] = (0.5 * (gr + gr.T)).astype(BF)
    dmat[1] = (0.5 * (gi - gi.T)).astype(BF)

    mine = jnp.where(r == c, 1.0, 0.0)
    hits = jnp.float32(0.0)
    for l in range(LEADS):
        hits = hits + jnp.where(jnp.logical_and(lead_slice[l] == r, lead_slot[l] == c), 1.0, 0.0)
    share_re = mine * dmat[1].astype(F32) - hits * inj[0].astype(F32)
    share_im = -mine * dmat[0].astype(F32) - hits * inj[1].astype(F32)
    msum[0] = share_re.astype(BF).reshape(4, 64, S)
    msum[1] = share_im.astype(BF).reshape(4, 64, S)
    to_mate = remote(msum.at[1 - core], m_in, m_send, m_recv, dev(r, c_mate))
    to_mate.start()

    cs, qs = col_copies(0, field.at[0])

    to_mate.wait_recv()
    msum[core] = (msum[core].astype(F32) + m_in[...].astype(F32)).astype(BF)
    scatter, gather = [], []
    for i in range(1, 4):
        peer = dev(r, col(hi, x + i, core))
        scatter.append(remote(msum.at[core, (x + i) % 4], rs_in.at[i - 1], rs_send.at[i - 1], rs_recv.at[i - 1], peer))
        quarter = lrow.at[core, x]
        gather.append(remote(quarter, quarter, ag_send.at[i - 1], ag_recv.at[i - 1], peer))
    for copy in scatter:
        copy.start()

    lands = (crow, cprev)
    h_copies = []
    for j, root in enumerate(roots):
        for u in range(2):
            rows = pl.ds(128 * u, 128)
            i = 2 * j + u

            def send(kind, on, p, to):
                copy = remote(coup.at[p, rows], lands[j].at[p, rows], h_send.at[6 * i + kind], h_recv.at[i], to)
                h_copies.append((on, copy))

                @pl.when(on)
                def _():
                    copy.start()

            to = root["to"]
            send(0, root["own"], 0, dev(to, col(hi, x + 1, 0)))
            send(1, root["own"], 1, dev(to, col(hi, x - 1, 1)))
            send(2, root["own"], 1 - core, dev(to, c_mate))
            send(3, root["far_re"], 0, dev(to, col(1 - hi, x, 0)))
            send(4, root["far_im"], 1, dev(to, col(1 - hi, x, 1)))

        @pl.when(root["own"])
        def _():
            lands[j][core] = coup[core]

    onward = []
    for j in range(2):
        for u in range(2):
            i = 2 * j + u
            place = lands[j].at[core, pl.ds(128 * u, 128)]
            copy = remote(place, place, h_send.at[6 * i + 5], h_recv.at[i], dev(r, col(hi, x + way, core)))
            onward.append(copy)
            h_copies.append((rings[j]["passes"], copy))

    def pass_on(j, level):
        @pl.when(jnp.logical_and(rings[j]["passes"], rings[j]["level"] == level))
        def _():
            for copy in onward[2 * j : 2 * j + 2]:
                copy.wait_recv()
                copy.start()

    def product_right(g, fr, fi):
        cr, ci = coup[0], coup[1]
        q_out[g, 0] = (nt(fr, ci) - nt(fi, cr)).astype(BF)
        q_out[g, 1] = (nt(fr, cr) + nt(fi, ci)).astype(BF)

    fr, fi = full(field.at[0])
    product_right(0, fr, fi)

    def forward(y, onto):
        y.wait_recv()

        @pl.when(gives_far)
        def _():
            onto.start()

    @pl.when(z < 7)
    def _():
        pl.semaphore_wait(near_sem, 1)

    def pieces_in():
        drain(kall.at[pl.ds(0, 7)], k_recv)
        swap.start()

    eight = pl.ds(8 * core, 8)
    swap = remote(kall.at[eight], kall.at[eight], s_send.at[3], s_recv.at[3], dev(r, c_mate))
    forward(ys[0], zs[0])
    ys[2].start()
    pieces_in()
    pass_on(0, 1)
    for copy in scatter:
        copy.wait_recv()
    total = msum[core, x].astype(F32)
    for i in range(3):
        total = total + rs_in[i].astype(F32)
    y_sum[...] = total.astype(BF)
    cross = remote(y_sum, y_in, hi_send, hi_recv, dev(r, (c + 8) % 16))
    cross.start()

    @pl.when(c > 0)
    def _():
        cs.start()

    @pl.when(c < 15)
    def _():
        qs.start()

    pass_on(1, 1)
    forward(ys[1], zs[1])
    ys[3].start()

    swap.wait_recv()
    sum_re = jnp.zeros((PIECE, S), F32)
    sum_im = jnp.zeros((PIECE, S), F32)
    for l in range(LEADS):
        slot = lead_slot[l]
        block = kall[8 * (slot % 2) + slot // 2].astype(F32)
        hit = jnp.where(lead_slice[l] == c, 1.0, 0.0)
        sum_re = sum_re + hit * block[0]
        sum_im = sum_im + hit * block[1]
    kcol[r, 0] = sum_re.astype(BF)
    kcol[r, 1] = sum_im.astype(BF)
    ay = remote(kcol.at[r], kcol.at[r], ay_send, ay_recv, dev(partner, c))
    ay.start()
    pass_on(0, 2)
    forward(ys[2], zs[2])
    pass_on(1, 2)
    ay.wait_recv()
    pair = pl.ds(r - y_lo, 2)

    @pl.when(z < 6)
    def _():
        pl.semaphore_wait(far_sem, 6 - z)

    @pl.loop(1, 8)
    def _(i):
        remote(kcol.at[pair], kcol.at[pair], a_send, a_recv, dev((r + 2 * i) % 16, c)).start()

    forward(ys[3], zs[3])
    cross.wait_recv()
    lrow[core, x] = (y_sum[...].astype(F32) + y_in[...].astype(F32)).astype(BF)
    for copy in gather:
        copy.start()

    pass_on(0, 3)
    pass_on(1, 3)

    g_rows = deph[pl.ds(pl.multiple_of(r * S, S), S)].reshape(1, S)
    g_cols = deph[pl.ds(pl.multiple_of(c * S, S), S)].reshape(1, S)
    wide = jnp.broadcast_to(g_rows, (S, S)).T + jnp.broadcast_to(g_cols, (S, S))
    ii = lax.broadcasted_iota(jnp.int32, (S, S), 0) + r * S
    jj = lax.broadcasted_iota(jnp.int32, (S, S), 1) + c * S
    rate[...] = jnp.where(ii == jj, 0.0, 0.5 * wide)

    def local_terms(own_re, own_im, fr, fi):
        dr, di = dmat[0], dmat[1]
        acc[0] = -rate[...] * own_re - nn(fr, di) - nn(fi, dr)
        acc[1] = -rate[...] * own_im + nn(fr, dr) - nn(fi, di)

    local_terms(rho[0], rho[1], fr, fi)

    shares = []
    for j, land in enumerate(lands):
        for u in range(2):
            @pl.when(jnp.logical_and(c != rings[j]["q"], jnp.logical_not(rings[j]["passes"])))
            def _():
                part_of = land.at[0, pl.ds(128 * u, 128)]
                pltpu.make_async_copy(part_of, part_of, h_recv.at[2 * j + u]).wait()

        share = remote(land.at[core], land.at[core], s_send.at[j], s_recv.at[j], dev(r, c_mate))
        share.start()
        shares.append(share)

    for copy in gather:
        copy.wait_recv()
    share = remote(lrow.at[core], lrow.at[core], s_send.at[2], s_recv.at[2], dev(r, c_mate))
    share.start()
    shares.append(share)

    def add_right(g):
        @pl.when(c < 15)
        def _():
            cs.wait_recv()

        nr, ni = full(right.at[g])
        cr, ci = coup[0], coup[1]
        acc[0] -= nn(nr, ci) + nn(ni, cr)
        acc[1] += nn(nr, cr) - nn(ni, ci)

    def add_q(g):
        @pl.when(c > 0)
        def _():
            qs.wait_recv()

        acc[0] += q_in[g, 0].astype(F32)
        acc[1] += q_in[g, 1].astype(F32)

    add_right(0)
    add_q(0)

    shares[0].wait_recv()
    shares[1].wait_recv()
    has_prior = jnp.where(r > 0, 1.0, 0.0).astype(BF)
    minus_prior = jnp.where(r > 0, -1.0, 0.0).astype(BF)
    minus_next = jnp.where(r < 15, -1.0, 0.0).astype(BF)

    def place(to_prior, to_next):
        to_prior[0] = has_prior * cprev[1]
        to_prior[1] = minus_prior * cprev[0]
        to_next[0] = minus_next * crow[1].T
        to_next[1] = minus_next * crow[0].T

    @pl.when(y_lo == 0)
    def _():
        place(l_far, l_part)

    @pl.when(y_lo == 1)
    def _():
        place(l_part, l_far)

    def left(lr, li, fr, fi):
        return nn(lr, fr) - nn(li, fi), nn(lr, fi) + nn(li, fr)

    def add_left(h, lr, li, fr, fi):
        more = left(lr, li, fr, fi)
        span = slice(h * HALF, (h + 1) * HALF)
        acc[0, :, span] += more[0]
        acc[1, :, span] += more[1]

    for h in range(2):
        add_left(h, l_part[0], l_part[1], part[0, h, 0], part[0, h, 1])

    shares[2].wait_recv()
    lr, li = lrow[0].reshape(S, S), lrow[1].reshape(S, S)
    more = left(lr, li, fr, fi)
    acc[0] += more[0]
    acc[1] += more[1]

    ys2, zs2 = row_copies(1)
    for h in range(2):
        @pl.when(gets_far)
        def _():
            zs[2 * h].wait_recv()
            zs[2 * h + 1].wait_recv()

        more = left(l_far[0], l_far[1], far[0, h, 0], far[0, h, 1])
        span = slice(h * HALF, (h + 1) * HALF)
        for p in range(2):
            value = step_scale * (acc[p, :, span] + more[p])
            phi[p, :, span] = value
            field[1, h, p] = value.astype(BF)
            ys2[2 * h + p].start()

    drain(kcol.at[pl.ds(0, 14)], a_recv)

    def lead_right(fr, fi):
        kr, ki = kcol[:, 0].reshape(S, S), kcol[:, 1].reshape(S, S)
        return step_scale * (nt(fr, kr) + nt(fi, ki)), step_scale * (nt(fi, kr) - nt(fr, ki))

    less = lead_right(fr, fi)
    phi[0] = phi[0] - less[0]
    phi[1] = phi[1] - less[1]
    halves(own, phi[0].astype(BF), phi[1].astype(BF))
    cs0, qs0 = cs, qs
    cs, qs = col_copies(1, own)

    @pl.when(c > 0)
    def _():
        cs.start()

    gr, gi = full(own)
    product_right(1, gr, gi)

    @pl.when(c < 15)
    def _():
        qs.start()

    fix[0], fix[1] = lead_right(*full(part.at[0]))
    forward(ys2[0], zs2[0])
    fix[2], fix[3] = lead_right(*full(far.at[0]))
    forward(ys2[1], zs2[1])
    local_terms(phi[0], phi[1], gr, gi)
    less = lead_right(gr, gi)
    more = left(lr, li, gr, gi)
    for p in range(2):
        acc[p] += more[p] - less[p] * (1.0 / step_scale)
    forward(ys2[2], zs2[2])
    forward(ys2[3], zs2[3])

    def corrected(ref, k, h):
        span = slice(h * HALF, (h + 1) * HALF)
        return [(ref[1, h, p].astype(F32) - fix[k + p, :, span]).astype(BF) for p in range(2)]

    @pl.when(c < 15)
    def _():
        cs.wait_recv()

    nr, ni = full(right.at[1])
    cr, ci = coup[0], coup[1]
    acc[0] -= nn(nr, ci) + nn(ni, cr)
    acc[1] += nn(nr, cr) - nn(ni, ci)

    @pl.when(c > 0)
    def _():
        qs.wait_recv()

    for p in range(2):
        acc[p] += q_in[1, p].astype(F32)
    for h in range(2):
        add_left(h, l_part[0], l_part[1], *corrected(part, 0, h))
    for p in range(2):
        acc[p] = (
            coeff_one * phi[p] + (2.0 * coeff_two * step_scale) * acc[p]
        )
    for h in range(2):
        @pl.when(gets_far)
        def _():
            zs2[2 * h].wait_recv()
            zs2[2 * h + 1].wait_recv()

        more = left(l_far[0], l_far[1], *corrected(far, 2, h))
        span = slice(h * HALF, (h + 1) * HALF)
        for p in range(2):
            out = (out_re, out_im)[p]
            out[:, span] = acc[p, :, span] + (2.0 * coeff_two * step_scale) * more[p]

    for copies in (ys, ys2, shares, scatter, gather, (swap, ay, to_mate, cross)):
        for one in copies:
            one.wait_send()

    @pl.when(gives_far)
    def _():
        for one in zs + zs2:
            one.wait_send()

    @pl.when(c > 0)
    def _():
        cs0.wait_send()
        cs.wait_send()

    @pl.when(c < 15)
    def _():
        qs0.wait_send()
        qs.wait_send()

    drain(kall.at[pl.ds(0, 7)], k_send)
    drain(kcol.at[pl.ds(0, 14)], a_send)

    for on, copy in h_copies:
        @pl.when(on)
        def _():
            copy.wait_send()


def shards(*args):
    hbm = pl.BlockSpec(memory_space=pl.ANY)
    dma = pltpu.SemaphoreType.DMA

    def blocks(*n):
        return pltpu.VMEM((*n, S, S), BF)

    def split(*n):
        return pltpu.VMEM((*n, 2, 2, S, HALF), BF)

    def quarters(*n):
        return pltpu.VMEM((*n, 64, S), BF)

    pieces = (16, 2, PIECE, S)
    outs = pl.pallas_call(
        kernel,
        name="propagate",
        out_shape=[jax.ShapeDtypeStruct((S, S), F32)] * 2,
        in_specs=[hbm] * 11,
        out_specs=[pl.BlockSpec(memory_space=pltpu.VMEM)] * 2,
        scratch_shapes=[
            pltpu.VMEM((2, S, S), F32), blocks(2), blocks(2), blocks(2), pltpu.VMEM((16 * S,), F32),
            pltpu.SMEM((LEADS,), jnp.int32), pltpu.SMEM((LEADS,), jnp.int32),
            split(2), split(2), split(2), split(), split(2), blocks(2, 2), blocks(2, 2),
            pltpu.VMEM((2, PIECE, S), BF), pltpu.VMEM(pieces, BF), blocks(2),
            pltpu.VMEM(pieces, BF), quarters(2, 4), quarters(4), quarters(3), quarters(), quarters(), quarters(2, 4),
            blocks(2), blocks(2), blocks(2), blocks(2),
            pltpu.VMEM((S, S), F32), pltpu.VMEM((2, S, S), F32), pltpu.VMEM((2, S, S), F32), pltpu.VMEM((4, S, S), F32),
            dma((13,)),
            dma((8,)), dma((8,)), dma((8,)), dma((8,)), dma((2,)), dma((2,)), dma((2,)), dma((2,)),
            dma, dma, dma, dma, dma, dma, dma((24,)), dma((4,)), dma((4,)), dma((4,)),
            pltpu.SemaphoreType.REGULAR, pltpu.SemaphoreType.REGULAR,
            dma, dma, dma((3,)), dma((3,)), dma, dma, dma((3,)), dma((3,)),
        ],
        compiler_params=pltpu.CompilerParams(
            collective_id=0, has_side_effects=True, vmem_limit_bytes=60 << 20
        ),
    )(*args)
    return tuple(o + (coeff_zero - coeff_two) * a for o, a in zip(outs, args))


def solution(mesh):
    return jax.shard_map(
        shards,
        mesh=mesh,
        in_specs=(
            P("row", "col"), P("row", "col"),
            P("col", None, None), P("col", None, None), P("col", None, None), P("col", None, None),
            P("col", None, None), P("col", None, None),
            P(), P(), P(),
        ),
        out_specs=(P("row", "col"), P("row", "col")),
        check_vma=False,
    )
```

```python
import jax
import jax.numpy as jnp
from jax import lax
from jax.experimental import pallas as pl
from jax.experimental.pallas import tpu as pltpu
from jax.sharding import PartitionSpec as P

S = 256
LEADS = 4
PIECE = 16

step_scale = 0.25
coeff_zero = 0.7652
coeff_one = 0.8801
coeff_two = 0.2298

BF = jnp.bfloat16
F32 = jnp.float32
MESH = pl.DeviceIdType.MESH


def nn(a, b):
    return jnp.dot(a, b, preferred_element_type=F32)


def nt(a, b):
    return lax.dot_general(a, b, (((1,), (1,)), ((), ())), preferred_element_type=F32)


HALF = 128


def kernel(
    rho_re_hbm, rho_im_hbm, diag_re_hbm, diag_im_hbm, coup_re_hbm, coup_im_hbm, inj_re_hbm, inj_im_hbm,
    deph_hbm, lead_slice_hbm, lead_slot_hbm,
    out_re, out_im,
    rho, diag, coup, inj, deph, lead_slice, lead_slot,
    field, part, far, own, right, q_out, q_in,
    kmine, kall, dmat, kcol, msum, m_in, rs_in, y_sum, y_in, lrow, crow, cprev, l_part, l_far, rate, acc, phi, fix,
    in_sem,
    y_send, y_recv, z_send, z_recv, c_send, c_recv, q_send, q_recv,
    k_send, k_recv, ay_send, ay_recv, a_send, a_recv, h_send, h_recv, s_send, s_recv,
    near_sem, far_sem, m_send, m_recv, rs_send, rs_recv, hi_send, hi_recv, ag_send, ag_recv,
):
    r = lax.axis_index("row")
    c = lax.axis_index("col")
    core = c % 2
    y_lo = r % 2
    partner = r + 1 - 2 * y_lo
    relay = (r + 2 - 4 * y_lo + 16) % 16
    c_mate = c + 1 - 2 * core
    c_out = c - 1 + 2 * core
    has_out = jnp.logical_and(c_out >= 0, c_out < 16)

    def dev(a, b):
        return {"row": a, "col": b}

    def local(src, dst, i):
        return pltpu.make_async_copy(src, dst, in_sem.at[i])

    rows16 = pl.ds(pl.multiple_of(r * PIECE, PIECE), PIECE)
    loads = [
        local(inj_re_hbm.at[0, rows16, :], kmine.at[0], 0),
        local(inj_im_hbm.at[0, rows16, :], kmine.at[1], 1),
        local(rho_re_hbm, rho.at[0], 2),
        local(rho_im_hbm, rho.at[1], 3),
        local(coup_re_hbm.at[0], coup.at[0], 4),
        local(coup_im_hbm.at[0], coup.at[1], 5),
        local(diag_re_hbm.at[0], diag.at[0], 6),
        local(diag_im_hbm.at[0], diag.at[1], 7),
        local(deph_hbm, deph, 8),
        local(lead_slice_hbm, lead_slice, 9),
        local(lead_slot_hbm, lead_slot, 10),
        local(inj_re_hbm.at[0], inj.at[0], 11),
        local(inj_im_hbm.at[0], inj.at[1], 12),
    ]
    for load in loads:
        load.start()

    z, x, hi = r // 2, (c // 2) % 4, c // 8
    way = 1 - 2 * core

    def col(hi, x, core):
        return 8 * hi + 2 * ((x + 8) % 4) + core

    def beside(z, y_lo):
        return jnp.where(y_lo == 0, jnp.where(z < 7, z + 1, 6), jnp.where(z > 0, z - 1, 1))

    z_side = beside(z, y_lo)
    gives_far = jnp.where(y_lo == 0, z, 7 - z) < 7
    gets_far = jnp.where(y_lo == 0, z, 7 - z) > 0
    rings = []
    for j in range(2):
        q = (r + 16 - j) % 16
        dist = ((x - (q // 2) % 4) * way + 8) % 4
        near = hi == q // 8
        start_far = jnp.where(core == 0, r + 1 - 2 * y_lo, 2 * z_side + 1 - y_lo)
        rings.append(dict(
            q=q,
            enters=jnp.logical_and(dist == 0, jnp.logical_not(near)),
            level=dist + jnp.where(near, 0, 1),
            first=jnp.logical_and(dist == 1, near),
            start_far=start_far,
            passes=jnp.logical_and(dist < 3, jnp.logical_or(dist > 0, jnp.logical_not(near))),
        ))
    roots = []
    for j in range(2):
        to = (c + j) % 16
        to_lo = to % 2
        other = beside(to // 2, to_lo)
        roots.append(dict(
            to=to,
            own=r == to,
            far_re=r == to + 1 - 2 * to_lo,
            far_im=r == 2 * other + 1 - to_lo,
        ))

    barrier = pltpu.get_barrier_semaphore()

    def greet(a, b):
        pl.semaphore_signal(barrier, inc=1, device_id=dev(a, b), device_id_type=MESH)

    for ring in rings:
        @pl.when(ring["enters"])
        def _():
            greet(ring["start_far"], ring["q"])

        @pl.when(ring["first"])
        def _():
            greet(r, ring["q"])

    @pl.loop(1, 8)
    def _(i):
        greet(r, (c + 2 * i) % 16)

        @pl.when(z + i < 8)
        def _():
            greet((r + 2 * i) % 16, c)

    @pl.when(has_out)
    def _():
        greet(r, c_out)

    greet(partner, c)
    greet(r, c_mate)

    for load in loads[:4]:
        load.wait()
    kslot = 8 * core + c // 2
    kall[kslot] = kmine[...]

    def halves(ref, value_re, value_im):
        for p, value in enumerate((value_re, value_im)):
            for h in range(2):
                ref[h, p] = value[:, h * HALF : (h + 1) * HALF]

    halves(field.at[0], rho[0].astype(BF), rho[1].astype(BF))

    @pl.when(c == 15)
    def _():
        right[...] = jnp.zeros_like(right)

    @pl.when(c == 0)
    def _():
        q_in[...] = jnp.zeros_like(q_in)

    @pl.when(jnp.logical_not(gets_far))
    def _():
        far[...] = jnp.zeros_like(far)

    sends_h = sum(
        jnp.where(t["own"], 2, 0) + jnp.where(t["far_re"], 1, 0) + jnp.where(t["far_im"], 1, 0) for t in roots
    )
    pl.semaphore_wait(barrier, 2 + jnp.where(has_out, 1, 0) + 7 + z + sends_h)

    def answer(sem, by):
        pl.semaphore_signal(sem, inc=1, device_id=dev((r + 16 - 2 * by) % 16, c), device_id_type=MESH)

    @pl.when(z > 0)
    def _():
        answer(near_sem, 1)

    @pl.loop(2, 8)
    def _(i):
        @pl.when(i <= z)
        def _():
            answer(far_sem, i)

    def remote(src, dst, ss, rs, to):
        return pltpu.make_async_remote_copy(
            src_ref=src, dst_ref=dst, send_sem=ss, recv_sem=rs, device_id=to, device_id_type=MESH
        )

    def drain(ref, sem):
        pltpu.make_async_copy(ref, ref, sem).wait()

    def row_copies(g):
        ys, zs = [], []
        for h in range(2):
            for p in range(2):
                i = 4 * g + 2 * h + p
                ys.append(remote(field.at[g, h, p], part.at[g, h, p], y_send.at[i], y_recv.at[i], dev(partner, c)))
                zs.append(remote(part.at[g, h, p], far.at[g, h, p], z_send.at[i], z_recv.at[i], dev(relay, c)))
        return ys, zs

    def col_copies(g, src):
        cs = remote(src, right.at[g], c_send.at[g], c_recv.at[g], dev(r, c - 1))
        qs = remote(q_out.at[g], q_in.at[g], q_send.at[g], q_recv.at[g], dev(r, c + 1))
        return cs, qs

    def full(ref):
        return (
            jnp.concatenate([ref[0, 0], ref[1, 0]], axis=1),
            jnp.concatenate([ref[0, 1], ref[1, 1]], axis=1),
        )

    @pl.loop(1, 8)
    def _(i):
        remote(kmine, kall.at[kslot], k_send, k_recv, dev(r, (c + 2 * i) % 16)).start()

    ys, zs = row_copies(0)
    ys[0].start()
    ys[1].start()
    for load in loads[4:]:
        load.wait()

    lands = (crow, cprev)
    h_copies = []
    for j, root in enumerate(roots):
        for u in range(2):
            rows = pl.ds(128 * u, 128)
            i = 2 * j + u

            def send(kind, on, p, to):
                copy = remote(coup.at[p, rows], lands[j].at[p, rows], h_send.at[6 * i + kind], h_recv.at[i], to)
                h_copies.append((on, copy))

                @pl.when(on)
                def _():
                    copy.start()

            to = root["to"]
            send(0, root["own"], 0, dev(to, col(hi, x + 1, 0)))
            send(1, root["own"], 1, dev(to, col(hi, x - 1, 1)))
            send(2, root["own"], 1 - core, dev(to, c_mate))
            send(3, root["far_re"], 0, dev(to, col(1 - hi, x, 0)))
            send(4, root["far_im"], 1, dev(to, col(1 - hi, x, 1)))

        @pl.when(root["own"])
        def _():
            lands[j][core] = coup[core]

    gr = diag[0].astype(F32)
    gi = diag[1].astype(F32)
    dmat[0] = (0.5 * (gr + gr.T)).astype(BF)
    dmat[1] = (0.5 * (gi - gi.T)).astype(BF)

    mine = jnp.where(r == c, 1.0, 0.0)
    hits = jnp.float32(0.0)
    for l in range(LEADS):
        hits = hits + jnp.where(jnp.logical_and(lead_slice[l] == r, lead_slot[l] == c), 1.0, 0.0)
    share_re = mine * dmat[1].astype(F32) - hits * inj[0].astype(F32)
    share_im = -mine * dmat[0].astype(F32) - hits * inj[1].astype(F32)
    msum[0] = share_re.astype(BF).reshape(4, 64, S)
    msum[1] = share_im.astype(BF).reshape(4, 64, S)
    to_mate = remote(msum.at[1 - core], m_in, m_send, m_recv, dev(r, c_mate))
    to_mate.start()

    cs, qs = col_copies(0, field.at[0])

    to_mate.wait_recv()
    msum[core] = (msum[core].astype(F32) + m_in[...].astype(F32)).astype(BF)
    scatter, gather = [], []
    for i in range(1, 4):
        peer = dev(r, col(hi, x + i, core))
        scatter.append(remote(msum.at[core, (x + i) % 4], rs_in.at[i - 1], rs_send.at[i - 1], rs_recv.at[i - 1], peer))
        quarter = lrow.at[core, x]
        gather.append(remote(quarter, quarter, ag_send.at[i - 1], ag_recv.at[i - 1], peer))
    for copy in scatter:
        copy.start()

    onward = []
    for j in range(2):
        for u in range(2):
            i = 2 * j + u
            place = lands[j].at[core, pl.ds(128 * u, 128)]
            copy = remote(place, place, h_send.at[6 * i + 5], h_recv.at[i], dev(r, col(hi, x + way, core)))
            onward.append(copy)
            h_copies.append((rings[j]["passes"], copy))

    def pass_on(j, level):
        @pl.when(jnp.logical_and(rings[j]["passes"], rings[j]["level"] == level))
        def _():
            for copy in onward[2 * j : 2 * j + 2]:
                copy.wait_recv()
                copy.start()

    def product_right(g, fr, fi):
        cr, ci = coup[0], coup[1]
        q_out[g, 0] = (nt(fr, ci) - nt(fi, cr)).astype(BF)
        q_out[g, 1] = (nt(fr, cr) + nt(fi, ci)).astype(BF)

    fr, fi = full(field.at[0])
    product_right(0, fr, fi)

    def forward(y, onto):
        y.wait_recv()

        @pl.when(gives_far)
        def _():
            onto.start()

    @pl.when(z < 7)
    def _():
        pl.semaphore_wait(near_sem, 1)

    def pieces_in():
        drain(kall.at[pl.ds(0, 7)], k_recv)
        swap.start()

    eight = pl.ds(8 * core, 8)
    swap = remote(kall.at[eight], kall.at[eight], s_send.at[4], s_recv.at[4], dev(r, c_mate))
    forward(ys[0], zs[0])
    ys[2].start()
    pieces_in()
    pass_on(0, 1)
    for copy in scatter:
        copy.wait_recv()
    total = msum[core, x].astype(F32)
    for i in range(3):
        total = total + rs_in[i].astype(F32)
    y_sum[...] = total.astype(BF)
    cross = remote(y_sum, y_in, hi_send, hi_recv, dev(r, (c + 8) % 16))
    cross.start()

    @pl.when(c > 0)
    def _():
        cs.start()

    @pl.when(c < 15)
    def _():
        qs.start()

    pass_on(1, 1)
    forward(ys[1], zs[1])
    ys[3].start()

    swap.wait_recv()
    sum_re = jnp.zeros((PIECE, S), F32)
    sum_im = jnp.zeros((PIECE, S), F32)
    for l in range(LEADS):
        slot = lead_slot[l]
        block = kall[8 * (slot % 2) + slot // 2].astype(F32)
        hit = jnp.where(lead_slice[l] == c, 1.0, 0.0)
        sum_re = sum_re + hit * block[0]
        sum_im = sum_im + hit * block[1]
    kcol[r, 0] = sum_re.astype(BF)
    kcol[r, 1] = sum_im.astype(BF)
    ay = remote(kcol.at[r], kcol.at[r], ay_send, ay_recv, dev(partner, c))
    ay.start()
    pass_on(0, 2)
    forward(ys[2], zs[2])
    pass_on(1, 2)
    ay.wait_recv()
    pair = pl.ds(r - y_lo, 2)

    @pl.when(z < 6)
    def _():
        pl.semaphore_wait(far_sem, 6 - z)

    @pl.loop(1, 8)
    def _(i):
        remote(kcol.at[pair], kcol.at[pair], a_send, a_recv, dev((r + 2 * i) % 16, c)).start()

    forward(ys[3], zs[3])
    cross.wait_recv()
    lrow[core, x] = (y_sum[...].astype(F32) + y_in[...].astype(F32)).astype(BF)
    for copy in gather:
        copy.start()

    pass_on(0, 3)
    pass_on(1, 3)

    g_rows = deph[pl.ds(pl.multiple_of(r * S, S), S)].reshape(1, S)
    g_cols = deph[pl.ds(pl.multiple_of(c * S, S), S)].reshape(1, S)
    wide = jnp.broadcast_to(g_rows, (S, S)).T + jnp.broadcast_to(g_cols, (S, S))
    ii = lax.broadcasted_iota(jnp.int32, (S, S), 0) + r * S
    jj = lax.broadcasted_iota(jnp.int32, (S, S), 1) + c * S
    rate[...] = jnp.where(ii == jj, 0.0, 0.5 * wide)

    def local_terms(own_re, own_im, fr, fi):
        dr, di = dmat[0], dmat[1]
        acc[0] = -rate[...] * own_re - nn(fr, di) - nn(fi, dr)
        acc[1] = -rate[...] * own_im + nn(fr, dr) - nn(fi, di)

    local_terms(rho[0], rho[1], fr, fi)

    shares = []
    for j, land in enumerate(lands):
        for u in range(2):
            part_of = land.at[core, pl.ds(128 * u, 128)]

            @pl.when(jnp.logical_and(c != rings[j]["q"], jnp.logical_not(rings[j]["passes"])))
            def _():
                pltpu.make_async_copy(part_of, part_of, h_recv.at[2 * j + u]).wait()

            share = remote(part_of, part_of, s_send.at[2 * j + u], s_recv.at[2 * j + u], dev(r, c_mate))
            share.start()
            shares.append(share)

    for copy in gather:
        copy.wait_recv()
    share = remote(lrow.at[core], lrow.at[core], s_send.at[5], s_recv.at[5], dev(r, c_mate))
    share.start()
    shares.append(share)

    def add_right(g):
        @pl.when(c < 15)
        def _():
            cs.wait_recv()

        nr, ni = full(right.at[g])
        cr, ci = coup[0], coup[1]
        acc[0] -= nn(nr, ci) + nn(ni, cr)
        acc[1] += nn(nr, cr) - nn(ni, ci)

    def add_q(g):
        @pl.when(c > 0)
        def _():
            qs.wait_recv()

        acc[0] += q_in[g, 0].astype(F32)
        acc[1] += q_in[g, 1].astype(F32)

    add_right(0)
    add_q(0)

    for i in range(4):
        shares[i].wait_recv()
    has_prior = jnp.where(r > 0, 1.0, 0.0).astype(BF)
    minus_prior = jnp.where(r > 0, -1.0, 0.0).astype(BF)
    minus_next = jnp.where(r < 15, -1.0, 0.0).astype(BF)

    def place(to_prior, to_next):
        to_prior[0] = has_prior * cprev[1]
        to_prior[1] = minus_prior * cprev[0]
        to_next[0] = minus_next * crow[1].T
        to_next[1] = minus_next * crow[0].T

    @pl.when(y_lo == 0)
    def _():
        place(l_far, l_part)

    @pl.when(y_lo == 1)
    def _():
        place(l_part, l_far)

    def left(lr, li, fr, fi):
        return nn(lr, fr) - nn(li, fi), nn(lr, fi) + nn(li, fr)

    def add_left(h, lr, li, fr, fi):
        more = left(lr, li, fr, fi)
        span = slice(h * HALF, (h + 1) * HALF)
        acc[0, :, span] += more[0]
        acc[1, :, span] += more[1]

    for h in range(2):
        add_left(h, l_part[0], l_part[1], part[0, h, 0], part[0, h, 1])

    shares[4].wait_recv()
    lr, li = lrow[0].reshape(S, S), lrow[1].reshape(S, S)
    more = left(lr, li, fr, fi)
    acc[0] += more[0]
    acc[1] += more[1]

    ys2, zs2 = row_copies(1)
    for h in range(2):
        @pl.when(gets_far)
        def _():
            zs[2 * h].wait_recv()
            zs[2 * h + 1].wait_recv()

        more = left(l_far[0], l_far[1], far[0, h, 0], far[0, h, 1])
        span = slice(h * HALF, (h + 1) * HALF)
        for p in range(2):
            value = step_scale * (acc[p, :, span] + more[p])
            phi[p, :, span] = value
            field[1, h, p] = value.astype(BF)
            ys2[2 * h + p].start()

    drain(kcol.at[pl.ds(0, 14)], a_recv)

    def lead_right(fr, fi):
        kr, ki = kcol[:, 0].reshape(S, S), kcol[:, 1].reshape(S, S)
        return step_scale * (nt(fr, kr) + nt(fi, ki)), step_scale * (nt(fi, kr) - nt(fr, ki))

    less = lead_right(fr, fi)
    phi[0] = phi[0] - less[0]
    phi[1] = phi[1] - less[1]
    halves(own, phi[0].astype(BF), phi[1].astype(BF))
    cs0, qs0 = cs, qs
    cs, qs = col_copies(1, own)

    @pl.when(c > 0)
    def _():
        cs.start()

    gr, gi = full(own)
    product_right(1, gr, gi)

    @pl.when(c < 15)
    def _():
        qs.start()

    fix[0], fix[1] = lead_right(*full(part.at[0]))
    forward(ys2[0], zs2[0])
    fix[2], fix[3] = lead_right(*full(far.at[0]))
    forward(ys2[1], zs2[1])
    local_terms(phi[0], phi[1], gr, gi)
    less = lead_right(gr, gi)
    more = left(lr, li, gr, gi)
    for p in range(2):
        acc[p] += more[p] - less[p] * (1.0 / step_scale)
    forward(ys2[2], zs2[2])
    forward(ys2[3], zs2[3])

    def corrected(ref, k, h):
        span = slice(h * HALF, (h + 1) * HALF)
        return [(ref[1, h, p].astype(F32) - fix[k + p, :, span]).astype(BF) for p in range(2)]

    @pl.when(c < 15)
    def _():
        cs.wait_recv()

    nr, ni = full(right.at[1])
    cr, ci = coup[0], coup[1]
    acc[0] -= nn(nr, ci) + nn(ni, cr)
    acc[1] += nn(nr, cr) - nn(ni, ci)

    @pl.when(c > 0)
    def _():
        qs.wait_recv()

    for p in range(2):
        acc[p] += q_in[1, p].astype(F32)
    for h in range(2):
        add_left(h, l_part[0], l_part[1], *corrected(part, 0, h))
    for p in range(2):
        acc[p] = (
            coeff_one * phi[p] + (2.0 * coeff_two * step_scale) * acc[p]
        )
    for h in range(2):
        @pl.when(gets_far)
        def _():
            zs2[2 * h].wait_recv()
            zs2[2 * h + 1].wait_recv()

        more = left(l_far[0], l_far[1], *corrected(far, 2, h))
        span = slice(h * HALF, (h + 1) * HALF)
        for p in range(2):
            out = (out_re, out_im)[p]
            out[:, span] = acc[p, :, span] + (2.0 * coeff_two * step_scale) * more[p]

    for copies in (ys, ys2, shares, scatter, gather, (swap, ay, to_mate, cross)):
        for one in copies:
            one.wait_send()

    @pl.when(gives_far)
    def _():
        for one in zs + zs2:
            one.wait_send()

    @pl.when(c > 0)
    def _():
        cs0.wait_send()
        cs.wait_send()

    @pl.when(c < 15)
    def _():
        qs0.wait_send()
        qs.wait_send()

    drain(kall.at[pl.ds(0, 7)], k_send)
    drain(kcol.at[pl.ds(0, 14)], a_send)

    for on, copy in h_copies:
        @pl.when(on)
        def _():
            copy.wait_send()


def shards(*args):
    hbm = pl.BlockSpec(memory_space=pl.ANY)
    dma = pltpu.SemaphoreType.DMA

    def blocks(*n):
        return pltpu.VMEM((*n, S, S), BF)

    def split(*n):
        return pltpu.VMEM((*n, 2, 2, S, HALF), BF)

    def quarters(*n):
        return pltpu.VMEM((*n, 64, S), BF)

    pieces = (16, 2, PIECE, S)
    outs = pl.pallas_call(
        kernel,
        name="propagate",
        out_shape=[jax.ShapeDtypeStruct((S, S), F32)] * 2,
        in_specs=[hbm] * 11,
        out_specs=[pl.BlockSpec(memory_space=pltpu.VMEM)] * 2,
        scratch_shapes=[
            pltpu.VMEM((2, S, S), F32), blocks(2), blocks(2), blocks(2), pltpu.VMEM((16 * S,), F32),
            pltpu.SMEM((LEADS,), jnp.int32), pltpu.SMEM((LEADS,), jnp.int32),
            split(2), split(2), split(2), split(), split(2), blocks(2, 2), blocks(2, 2),
            pltpu.VMEM((2, PIECE, S), BF), pltpu.VMEM(pieces, BF), blocks(2),
            pltpu.VMEM(pieces, BF), quarters(2, 4), quarters(4), quarters(3), quarters(), quarters(), quarters(2, 4),
            blocks(2), blocks(2), blocks(2), blocks(2),
            pltpu.VMEM((S, S), F32), pltpu.VMEM((2, S, S), F32), pltpu.VMEM((2, S, S), F32), pltpu.VMEM((4, S, S), F32),
            dma((13,)),
            dma((8,)), dma((8,)), dma((8,)), dma((8,)), dma((2,)), dma((2,)), dma((2,)), dma((2,)),
            dma, dma, dma, dma, dma, dma, dma((24,)), dma((4,)), dma((6,)), dma((6,)),
            pltpu.SemaphoreType.REGULAR, pltpu.SemaphoreType.REGULAR,
            dma, dma, dma((3,)), dma((3,)), dma, dma, dma((3,)), dma((3,)),
        ],
        compiler_params=pltpu.CompilerParams(
            collective_id=0, has_side_effects=True, vmem_limit_bytes=60 << 20
        ),
    )(*args)
    return tuple(o + (coeff_zero - coeff_two) * a for o, a in zip(outs, args))


def solution(mesh):
    return jax.shard_map(
        shards,
        mesh=mesh,
        in_specs=(
            P("row", "col"), P("row", "col"),
            P("col", None, None), P("col", None, None), P("col", None, None), P("col", None, None),
            P("col", None, None), P("col", None, None),
            P(), P(), P(),
        ),
        out_specs=(P("row", "col"), P("row", "col")),
        check_vma=False,
    )
```

```python
import jax
import jax.numpy as jnp
from jax import lax
from jax.experimental import pallas as pl
from jax.experimental.pallas import tpu as pltpu
from jax.sharding import PartitionSpec as P

S = 256
LEADS = 4
PIECE = 16

step_scale = 0.25
coeff_zero = 0.7652
coeff_one = 0.8801
coeff_two = 0.2298

BF = jnp.bfloat16
F32 = jnp.float32
MESH = pl.DeviceIdType.MESH


def nn(a, b):
    return jnp.dot(a, b, preferred_element_type=F32)


def nt(a, b):
    return lax.dot_general(a, b, (((1,), (1,)), ((), ())), preferred_element_type=F32)


HALF = 128


def kernel(
    rho_re_hbm, rho_im_hbm, diag_re_hbm, diag_im_hbm, coup_re_hbm, coup_im_hbm, inj_re_hbm, inj_im_hbm,
    deph_hbm, lead_slice_hbm, lead_slot_hbm,
    out_re, out_im,
    rho, diag, coup, inj, deph, lead_slice, lead_slot,
    field, part, far, own, right, q_out, q_in,
    kmine, kall, dmat, kcol, msum, m_in, rs_in, y_sum, y_in, lrow, crow, cprev, l_part, l_far, rate, acc, phi, fix,
    in_sem,
    y_send, y_recv, z_send, z_recv, c_send, c_recv, q_send, q_recv,
    k_send, k_recv, ay_send, ay_recv, a_send, a_recv, h_send, h_recv, s_send, s_recv,
    near_sem, far_sem, m_send, m_recv, rs_send, rs_recv, hi_send, hi_recv, ag_send, ag_recv,
):
    r = lax.axis_index("row")
    c = lax.axis_index("col")
    core = c % 2
    y_lo = r % 2
    partner = r + 1 - 2 * y_lo
    relay = (r + 2 - 4 * y_lo + 16) % 16
    c_mate = c + 1 - 2 * core
    c_out = c - 1 + 2 * core
    has_out = jnp.logical_and(c_out >= 0, c_out < 16)

    def dev(a, b):
        return {"row": a, "col": b}

    def local(src, dst, i):
        return pltpu.make_async_copy(src, dst, in_sem.at[i])

    rows16 = pl.ds(pl.multiple_of(r * PIECE, PIECE), PIECE)
    loads = [
        local(inj_re_hbm.at[0, rows16, :], kmine.at[0], 0),
        local(inj_im_hbm.at[0, rows16, :], kmine.at[1], 1),
        local(rho_re_hbm, rho.at[0], 2),
        local(rho_im_hbm, rho.at[1], 3),
        local(coup_re_hbm.at[0], coup.at[0], 4),
        local(coup_im_hbm.at[0], coup.at[1], 5),
        local(diag_re_hbm.at[0], diag.at[0], 6),
        local(diag_im_hbm.at[0], diag.at[1], 7),
        local(deph_hbm, deph, 8),
        local(lead_slice_hbm, lead_slice, 9),
        local(lead_slot_hbm, lead_slot, 10),
        local(inj_re_hbm.at[0], inj.at[0], 11),
        local(inj_im_hbm.at[0], inj.at[1], 12),
    ]
    for load in loads:
        load.start()

    z, x, hi = r // 2, (c // 2) % 4, c // 8
    way = 1 - 2 * core

    def col(hi, x, core):
        return 8 * hi + 2 * ((x + 8) % 4) + core

    def beside(z, y_lo):
        return jnp.where(y_lo == 0, jnp.where(z < 7, z + 1, 6), jnp.where(z > 0, z - 1, 1))

    z_side = beside(z, y_lo)
    gives_far = jnp.where(y_lo == 0, z, 7 - z) < 7
    gets_far = jnp.where(y_lo == 0, z, 7 - z) > 0
    rings = []
    for j in range(2):
        q = (r + 16 - j) % 16
        dist = ((x - (q // 2) % 4) * way + 8) % 4
        near = hi == q // 8
        start_far = jnp.where(core == 0, r + 1 - 2 * y_lo, 2 * z_side + 1 - y_lo)
        rings.append(dict(
            q=q,
            enters=jnp.logical_and(dist == 0, jnp.logical_not(near)),
            level=dist + jnp.where(near, 0, 1),
            first=jnp.logical_and(dist == 1, near),
            start_far=start_far,
            passes=jnp.logical_and(dist < 3, jnp.logical_or(dist > 0, jnp.logical_not(near))),
        ))
    roots = []
    for j in range(2):
        to = (c + j) % 16
        to_lo = to % 2
        other = beside(to // 2, to_lo)
        roots.append(dict(
            to=to,
            own=r == to,
            far_re=r == to + 1 - 2 * to_lo,
            far_im=r == 2 * other + 1 - to_lo,
        ))

    barrier = pltpu.get_barrier_semaphore()

    def greet(a, b):
        pl.semaphore_signal(barrier, inc=1, device_id=dev(a, b), device_id_type=MESH)

    for ring in rings:
        @pl.when(ring["enters"])
        def _():
            greet(ring["start_far"], ring["q"])

        @pl.when(ring["first"])
        def _():
            greet(r, ring["q"])

    @pl.loop(1, 8)
    def _(i):
        greet(r, (c + 2 * i) % 16)

        @pl.when(z + i < 8)
        def _():
            greet((r + 2 * i) % 16, c)

    @pl.when(has_out)
    def _():
        greet(r, c_out)

    greet(partner, c)
    greet(r, c_mate)

    for load in loads[:4]:
        load.wait()
    kslot = 8 * core + c // 2
    kall[kslot] = kmine[...]

    def halves(ref, value_re, value_im):
        for p, value in enumerate((value_re, value_im)):
            for h in range(2):
                ref[h, p] = value[:, h * HALF : (h + 1) * HALF]

    halves(field.at[0], rho[0].astype(BF), rho[1].astype(BF))

    @pl.when(c == 15)
    def _():
        right[...] = jnp.zeros_like(right)

    @pl.when(c == 0)
    def _():
        q_in[...] = jnp.zeros_like(q_in)

    @pl.when(jnp.logical_not(gets_far))
    def _():
        far[...] = jnp.zeros_like(far)

    sends_h = sum(
        jnp.where(t["own"], 2, 0) + jnp.where(t["far_re"], 1, 0) + jnp.where(t["far_im"], 1, 0) for t in roots
    )
    pl.semaphore_wait(barrier, 2 + jnp.where(has_out, 1, 0) + 7 + z + sends_h)

    def answer(sem, by):
        pl.semaphore_signal(sem, inc=1, device_id=dev((r + 16 - 2 * by) % 16, c), device_id_type=MESH)

    @pl.when(z > 0)
    def _():
        answer(near_sem, 1)

    @pl.loop(2, 8)
    def _(i):
        @pl.when(i <= z)
        def _():
            answer(far_sem, i)

    def remote(src, dst, ss, rs, to):
        return pltpu.make_async_remote_copy(
            src_ref=src, dst_ref=dst, send_sem=ss, recv_sem=rs, device_id=to, device_id_type=MESH
        )

    def drain(ref, sem):
        pltpu.make_async_copy(ref, ref, sem).wait()

    def row_copies(g):
        ys, zs = [], []
        for h in range(2):
            for p in range(2):
                i = 4 * g + 2 * h + p
                ys.append(remote(field.at[g, h, p], part.at[g, h, p], y_send.at[i], y_recv.at[i], dev(partner, c)))
                zs.append(remote(part.at[g, h, p], far.at[g, h, p], z_send.at[i], z_recv.at[i], dev(relay, c)))
        return ys, zs

    def col_copies(g, src):
        cs = remote(src, right.at[g], c_send.at[g], c_recv.at[g], dev(r, c - 1))
        qs = remote(q_out.at[g], q_in.at[g], q_send.at[g], q_recv.at[g], dev(r, c + 1))
        return cs, qs

    def full(ref):
        return (
            jnp.concatenate([ref[0, 0], ref[1, 0]], axis=1),
            jnp.concatenate([ref[0, 1], ref[1, 1]], axis=1),
        )

    @pl.loop(1, 8)
    def _(i):
        remote(kmine, kall.at[kslot], k_send, k_recv, dev(r, (c + 2 * i) % 16)).start()

    ys, zs = row_copies(0)
    for y in ys:
        y.start()
    for load in loads[4:6]:
        load.wait()

    lands = (crow, cprev)
    h_copies = []
    for j, root in enumerate(roots):
        for u in range(2):
            rows = pl.ds(128 * u, 128)
            i = 2 * j + u

            def send(kind, on, p, to):
                copy = remote(coup.at[p, rows], lands[j].at[p, rows], h_send.at[6 * i + kind], h_recv.at[i], to)
                h_copies.append((on, copy))

                @pl.when(on)
                def _():
                    copy.start()

            to = root["to"]
            send(0, root["own"], 0, dev(to, col(hi, x + 1, 0)))
            send(1, root["own"], 1, dev(to, col(hi, x - 1, 1)))
            send(2, root["own"], 1 - core, dev(to, c_mate))
            send(3, root["far_re"], 0, dev(to, col(1 - hi, x, 0)))
            send(4, root["far_im"], 1, dev(to, col(1 - hi, x, 1)))

        @pl.when(root["own"])
        def _():
            lands[j][core] = coup[core]

    for load in loads[6:]:
        load.wait()

    gr = diag[0].astype(F32)
    gi = diag[1].astype(F32)
    dmat[0] = (0.5 * (gr + gr.T)).astype(BF)
    dmat[1] = (0.5 * (gi - gi.T)).astype(BF)

    mine = jnp.where(r == c, 1.0, 0.0)
    hits = jnp.float32(0.0)
    for l in range(LEADS):
        hits = hits + jnp.where(jnp.logical_and(lead_slice[l] == r, lead_slot[l] == c), 1.0, 0.0)
    share_re = mine * dmat[1].astype(F32) - hits * inj[0].astype(F32)
    share_im = -mine * dmat[0].astype(F32) - hits * inj[1].astype(F32)
    msum[0] = share_re.astype(BF).reshape(4, 64, S)
    msum[1] = share_im.astype(BF).reshape(4, 64, S)
    to_mate = remote(msum.at[1 - core], m_in, m_send, m_recv, dev(r, c_mate))
    to_mate.start()

    cs, qs = col_copies(0, field.at[0])

    to_mate.wait_recv()
    msum[core] = (msum[core].astype(F32) + m_in[...].astype(F32)).astype(BF)
    scatter, gather = [], []
    for i in range(1, 4):
        peer = dev(r, col(hi, x + i, core))
        scatter.append(remote(msum.at[core, (x + i) % 4], rs_in.at[i - 1], rs_send.at[i - 1], rs_recv.at[i - 1], peer))
        quarter = lrow.at[core, x]
        gather.append(remote(quarter, quarter, ag_send.at[i - 1], ag_recv.at[i - 1], peer))
    for copy in scatter:
        copy.start()

    onward = []
    for j in range(2):
        for u in range(2):
            i = 2 * j + u
            place = lands[j].at[core, pl.ds(128 * u, 128)]
            copy = remote(place, place, h_send.at[6 * i + 5], h_recv.at[i], dev(r, col(hi, x + way, core)))
            onward.append(copy)
            h_copies.append((rings[j]["passes"], copy))

    def pass_on(j, level):
        @pl.when(jnp.logical_and(rings[j]["passes"], rings[j]["level"] == level))
        def _():
            for copy in onward[2 * j : 2 * j + 2]:
                copy.wait_recv()
                copy.start()

    def product_right(g, fr, fi):
        cr, ci = coup[0], coup[1]
        q_out[g, 0] = (nt(fr, ci) - nt(fi, cr)).astype(BF)
        q_out[g, 1] = (nt(fr, cr) + nt(fi, ci)).astype(BF)

    fr, fi = full(field.at[0])
    product_right(0, fr, fi)

    def forward(y, onto):
        y.wait_recv()

        @pl.when(gives_far)
        def _():
            onto.start()

    @pl.when(z < 7)
    def _():
        pl.semaphore_wait(near_sem, 1)

    def pieces_in():
        drain(kall.at[pl.ds(0, 7)], k_recv)
        swap.start()

    eight = pl.ds(8 * core, 8)
    swap = remote(kall.at[eight], kall.at[eight], s_send.at[4], s_recv.at[4], dev(r, c_mate))
    forward(ys[0], zs[0])
    pieces_in()
    pass_on(0, 1)
    for copy in scatter:
        copy.wait_recv()
    total = msum[core, x].astype(F32)
    for i in range(3):
        total = total + rs_in[i].astype(F32)
    y_sum[...] = total.astype(BF)
    cross = remote(y_sum, y_in, hi_send, hi_recv, dev(r, (c + 8) % 16))
    cross.start()

    @pl.when(c > 0)
    def _():
        cs.start()

    @pl.when(c < 15)
    def _():
        qs.start()

    pass_on(1, 1)
    forward(ys[1], zs[1])

    swap.wait_recv()
    sum_re = jnp.zeros((PIECE, S), F32)
    sum_im = jnp.zeros((PIECE, S), F32)
    for l in range(LEADS):
        slot = lead_slot[l]
        block = kall[8 * (slot % 2) + slot // 2].astype(F32)
        hit = jnp.where(lead_slice[l] == c, 1.0, 0.0)
        sum_re = sum_re + hit * block[0]
        sum_im = sum_im + hit * block[1]
    kcol[r, 0] = sum_re.astype(BF)
    kcol[r, 1] = sum_im.astype(BF)
    ay = remote(kcol.at[r], kcol.at[r], ay_send, ay_recv, dev(partner, c))
    ay.start()
    pass_on(0, 2)
    forward(ys[2], zs[2])
    pass_on(1, 2)
    ay.wait_recv()
    pair = pl.ds(r - y_lo, 2)

    @pl.when(z < 6)
    def _():
        pl.semaphore_wait(far_sem, 6 - z)

    @pl.loop(1, 8)
    def _(i):
        remote(kcol.at[pair], kcol.at[pair], a_send, a_recv, dev((r + 2 * i) % 16, c)).start()

    forward(ys[3], zs[3])
    cross.wait_recv()
    lrow[core, x] = (y_sum[...].astype(F32) + y_in[...].astype(F32)).astype(BF)
    for copy in gather:
        copy.start()

    pass_on(0, 3)
    pass_on(1, 3)

    g_rows = deph[pl.ds(pl.multiple_of(r * S, S), S)].reshape(1, S)
    g_cols = deph[pl.ds(pl.multiple_of(c * S, S), S)].reshape(1, S)
    wide = jnp.broadcast_to(g_rows, (S, S)).T + jnp.broadcast_to(g_cols, (S, S))
    ii = lax.broadcasted_iota(jnp.int32, (S, S), 0) + r * S
    jj = lax.broadcasted_iota(jnp.int32, (S, S), 1) + c * S
    rate[...] = jnp.where(ii == jj, 0.0, 0.5 * wide)

    def local_terms(own_re, own_im, fr, fi):
        dr, di = dmat[0], dmat[1]
        acc[0] = -rate[...] * own_re - nn(fr, di) - nn(fi, dr)
        acc[1] = -rate[...] * own_im + nn(fr, dr) - nn(fi, di)

    local_terms(rho[0], rho[1], fr, fi)

    shares = []
    for j, land in enumerate(lands):
        for u in range(2):
            part_of = land.at[core, pl.ds(128 * u, 128)]

            @pl.when(jnp.logical_and(c != rings[j]["q"], jnp.logical_not(rings[j]["passes"])))
            def _():
                pltpu.make_async_copy(part_of, part_of, h_recv.at[2 * j + u]).wait()

            share = remote(part_of, part_of, s_send.at[2 * j + u], s_recv.at[2 * j + u], dev(r, c_mate))
            share.start()
            shares.append(share)

    for copy in gather:
        copy.wait_recv()
    share = remote(lrow.at[core], lrow.at[core], s_send.at[5], s_recv.at[5], dev(r, c_mate))
    share.start()
    shares.append(share)

    def add_right(g):
        @pl.when(c < 15)
        def _():
            cs.wait_recv()

        nr, ni = full(right.at[g])
        cr, ci = coup[0], coup[1]
        acc[0] -= nn(nr, ci) + nn(ni, cr)
        acc[1] += nn(nr, cr) - nn(ni, ci)

    def add_q(g):
        @pl.when(c > 0)
        def _():
            qs.wait_recv()

        acc[0] += q_in[g, 0].astype(F32)
        acc[1] += q_in[g, 1].astype(F32)

    add_right(0)
    add_q(0)

    for i in range(4):
        shares[i].wait_recv()
    has_prior = jnp.where(r > 0, 1.0, 0.0).astype(BF)
    minus_prior = jnp.where(r > 0, -1.0, 0.0).astype(BF)
    minus_next = jnp.where(r < 15, -1.0, 0.0).astype(BF)

    def place(to_prior, to_next):
        to_prior[0] = has_prior * cprev[1]
        to_prior[1] = minus_prior * cprev[0]
        to_next[0] = minus_next * crow[1].T
        to_next[1] = minus_next * crow[0].T

    @pl.when(y_lo == 0)
    def _():
        place(l_far, l_part)

    @pl.when(y_lo == 1)
    def _():
        place(l_part, l_far)

    def left(lr, li, fr, fi):
        return nn(lr, fr) - nn(li, fi), nn(lr, fi) + nn(li, fr)

    def add_left(h, lr, li, fr, fi):
        more = left(lr, li, fr, fi)
        span = slice(h * HALF, (h + 1) * HALF)
        acc[0, :, span] += more[0]
        acc[1, :, span] += more[1]

    for h in range(2):
        add_left(h, l_part[0], l_part[1], part[0, h, 0], part[0, h, 1])

    shares[4].wait_recv()
    lr, li = lrow[0].reshape(S, S), lrow[1].reshape(S, S)
    more = left(lr, li, fr, fi)
    acc[0] += more[0]
    acc[1] += more[1]

    ys2, zs2 = row_copies(1)
    for h in range(2):
        @pl.when(gets_far)
        def _():
            zs[2 * h].wait_recv()
            zs[2 * h + 1].wait_recv()

        more = left(l_far[0], l_far[1], far[0, h, 0], far[0, h, 1])
        span = slice(h * HALF, (h + 1) * HALF)
        for p in range(2):
            value = step_scale * (acc[p, :, span] + more[p])
            phi[p, :, span] = value
            field[1, h, p] = value.astype(BF)
            ys2[2 * h + p].start()

    drain(kcol.at[pl.ds(0, 14)], a_recv)

    def lead_right(fr, fi):
        kr, ki = kcol[:, 0].reshape(S, S), kcol[:, 1].reshape(S, S)
        return step_scale * (nt(fr, kr) + nt(fi, ki)), step_scale * (nt(fi, kr) - nt(fr, ki))

    less = lead_right(fr, fi)
    phi[0] = phi[0] - less[0]
    phi[1] = phi[1] - less[1]
    halves(own, phi[0].astype(BF), phi[1].astype(BF))
    cs0, qs0 = cs, qs
    cs, qs = col_copies(1, own)

    @pl.when(c > 0)
    def _():
        cs.start()

    gr, gi = full(own)
    product_right(1, gr, gi)

    @pl.when(c < 15)
    def _():
        qs.start()

    fix[0], fix[1] = lead_right(*full(part.at[0]))
    forward(ys2[0], zs2[0])
    fix[2], fix[3] = lead_right(*full(far.at[0]))
    forward(ys2[1], zs2[1])
    local_terms(phi[0], phi[1], gr, gi)
    less = lead_right(gr, gi)
    more = left(lr, li, gr, gi)
    for p in range(2):
        acc[p] += more[p] - less[p] * (1.0 / step_scale)
    forward(ys2[2], zs2[2])
    forward(ys2[3], zs2[3])

    def corrected(ref, k, h):
        span = slice(h * HALF, (h + 1) * HALF)
        return [(ref[1, h, p].astype(F32) - fix[k + p, :, span]).astype(BF) for p in range(2)]

    @pl.when(c < 15)
    def _():
        cs.wait_recv()

    nr, ni = full(right.at[1])
    cr, ci = coup[0], coup[1]
    acc[0] -= nn(nr, ci) + nn(ni, cr)
    acc[1] += nn(nr, cr) - nn(ni, ci)

    @pl.when(c > 0)
    def _():
        qs.wait_recv()

    for p in range(2):
        acc[p] += q_in[1, p].astype(F32)
    for h in range(2):
        add_left(h, l_part[0], l_part[1], *corrected(part, 0, h))
    for p in range(2):
        acc[p] = (
            coeff_one * phi[p] + (2.0 * coeff_two * step_scale) * acc[p]
        )
    for h in range(2):
        @pl.when(gets_far)
        def _():
            zs2[2 * h].wait_recv()
            zs2[2 * h + 1].wait_recv()

        more = left(l_far[0], l_far[1], *corrected(far, 2, h))
        span = slice(h * HALF, (h + 1) * HALF)
        for p in range(2):
            out = (out_re, out_im)[p]
            out[:, span] = acc[p, :, span] + (2.0 * coeff_two * step_scale) * more[p]

    for copies in (ys, ys2, shares, scatter, gather, (swap, ay, to_mate, cross)):
        for one in copies:
            one.wait_send()

    @pl.when(gives_far)
    def _():
        for one in zs + zs2:
            one.wait_send()

    @pl.when(c > 0)
    def _():
        cs0.wait_send()
        cs.wait_send()

    @pl.when(c < 15)
    def _():
        qs0.wait_send()
        qs.wait_send()

    drain(kall.at[pl.ds(0, 7)], k_send)
    drain(kcol.at[pl.ds(0, 14)], a_send)

    for on, copy in h_copies:
        @pl.when(on)
        def _():
            copy.wait_send()


def shards(*args):
    hbm = pl.BlockSpec(memory_space=pl.ANY)
    dma = pltpu.SemaphoreType.DMA

    def blocks(*n):
        return pltpu.VMEM((*n, S, S), BF)

    def split(*n):
        return pltpu.VMEM((*n, 2, 2, S, HALF), BF)

    def quarters(*n):
        return pltpu.VMEM((*n, 64, S), BF)

    pieces = (16, 2, PIECE, S)
    outs = pl.pallas_call(
        kernel,
        name="propagate",
        out_shape=[jax.ShapeDtypeStruct((S, S), F32)] * 2,
        in_specs=[hbm] * 11,
        out_specs=[pl.BlockSpec(memory_space=pltpu.VMEM)] * 2,
        scratch_shapes=[
            pltpu.VMEM((2, S, S), F32), blocks(2), blocks(2), blocks(2), pltpu.VMEM((16 * S,), F32),
            pltpu.SMEM((LEADS,), jnp.int32), pltpu.SMEM((LEADS,), jnp.int32),
            split(2), split(2), split(2), split(), split(2), blocks(2, 2), blocks(2, 2),
            pltpu.VMEM((2, PIECE, S), BF), pltpu.VMEM(pieces, BF), blocks(2),
            pltpu.VMEM(pieces, BF), quarters(2, 4), quarters(4), quarters(3), quarters(), quarters(), quarters(2, 4),
            blocks(2), blocks(2), blocks(2), blocks(2),
            pltpu.VMEM((S, S), F32), pltpu.VMEM((2, S, S), F32), pltpu.VMEM((2, S, S), F32), pltpu.VMEM((4, S, S), F32),
            dma((13,)),
            dma((8,)), dma((8,)), dma((8,)), dma((8,)), dma((2,)), dma((2,)), dma((2,)), dma((2,)),
            dma, dma, dma, dma, dma, dma, dma((24,)), dma((4,)), dma((6,)), dma((6,)),
            pltpu.SemaphoreType.REGULAR, pltpu.SemaphoreType.REGULAR,
            dma, dma, dma((3,)), dma((3,)), dma, dma, dma((3,)), dma((3,)),
        ],
        compiler_params=pltpu.CompilerParams(
            collective_id=0, has_side_effects=True, vmem_limit_bytes=60 << 20
        ),
    )(*args)
    return tuple(o + (coeff_zero - coeff_two) * a for o, a in zip(outs, args))


def solution(mesh):
    return jax.shard_map(
        shards,
        mesh=mesh,
        in_specs=(
            P("row", "col"), P("row", "col"),
            P("col", None, None), P("col", None, None), P("col", None, None), P("col", None, None),
            P("col", None, None), P("col", None, None),
            P(), P(), P(),
        ),
        out_specs=(P("row", "col"), P("row", "col")),
        check_vma=False,
    )
```
